128 devices in a mesh: dp: 32 (over z, x, y_lo), mp: 4 (over y_hi, core).
Axes of the slice: x: 4, y: 4 (y_hi: 2, y_lo: 2; y = y_hi * 2 + y_lo), z: 4, core: 2. Of those that a mesh axis runs over, the one named last changes fastest.
Arguments:
- tokens: bfloat16 [32, 512, 768], P('dp'), may hold values from -6 to 6
- segment_lens: int32 [32, 8], P('dp'), may hold values from 1 to 256, as said below
- norm1_gain: float32 [768], replicated, may hold values from 0.5 to 1.5
- norm1_shift: float32 [768], replicated, may hold values from -1.25 to 1.25
- qkv_weight: bfloat16 [768, 12, 192], P(None, 'mp'), may hold values from -0.21875 to 0.21875
- qv_bias: float32 [12, 128], P('mp'), may hold values from -1.25 to 1.25
- out_weight: bfloat16 [768, 768], P('mp'), may hold values from -1.25 to 1.25
- out_bias: float32 [768], replicated, may hold values from -1.25 to 1.25
- norm2_gain: float32 [768], replicated, may hold values from 0.5 to 1.5
- norm2_shift: float32 [768], replicated, may hold values from -1.25 to 1.25
- up_weight: bfloat16 [768, 3072], P(None, 'mp'), may hold values from -0.21875 to 0.21875
- up_bias: float32 [3072], P('mp'), may hold values from -1.25 to 1.25
- down_weight: bfloat16 [3072, 768], P('mp'), may hold values from -0.109375 to 0.109375
- down_bias: float32 [768], replicated, may hold values from -1.25 to 1.25
- cotangent: bfloat16 [32, 512, 768], P('dp'), may hold values from -6 to 6
Outputs:
- mixed: bfloat16 [32, 512, 768], P('dp')
- tokens_grad: float32 [32, 512, 768], P('dp')
- norm1_gain_grad: float32 [768], replicated
- norm1_shift_grad: float32 [768], replicated
- qkv_weight_grad: float32 [768, 12, 192], P(None, 'mp')
- qv_bias_grad: float32 [12, 128], P('mp')
- out_weight_grad: float32 [768, 768], P('mp')
- out_bias_grad: float32 [768], replicated
- norm2_gain_grad: float32 [768], replicated
- norm2_shift_grad: float32 [768], replicated
- up_weight_grad: float32 [768, 3072], P(None, 'mp')
- up_bias_grad: float32 [3072], P('mp')
- down_weight_grad: float32 [3072, 768], P('mp')
- down_bias_grad: float32 [768], replicated
The draws below stay inside these ranges and needn't reach their ends.
Inputs may be any that keep to these rules, and one draw needn't show every extreme that they name: `segment_lens`: each row's 8 document lengths are positive and sum to at most 512; the first row's sum to exactly 512, and its first document is exactly 256 long. Positions from that sum to the row's end form its padded tail.
All inputs are finite; a program needn't handle non-finite values.
Results may differ from the reference program's by a relative error of at most 0.028.
Values may be sent and summed in bfloat16 or wider, within the bound.
No kernel may reach another device: no remote copies, remote signals or barrier semaphores. Data moves between devices by JAX's collectives and lax.ppermute only.
A program may use at most 64 MiB of HBM per device.

```python
import jax
import jax.numpy as jnp
from jax import lax

D = 768
HEADS = 12
HD = 64
FF = 3072
SEQ = 512
SEGS = 8
ROWS = 32
N_MP = 4


def split_lengths(total, shares):
    running = jnp.cumsum(shares, axis=1)
    bounds = (total[:, None] * running // running[:, -1:]).astype(jnp.int32)
    starts = jnp.concatenate([jnp.zeros((shares.shape[0], 1), jnp.int32), bounds[:, :-1]], axis=1)
    return (bounds - starts).astype(jnp.int32)


def draw_segment_lens(key, part):
    key = jax.random.fold_in(key, 11)
    tail_key, weight_key = jax.random.split(key)
    tails = jax.random.randint(tail_key, (ROWS,), 0, SEQ // 4)
    tails = jnp.where(jnp.arange(ROWS) == 0, 0, tails)
    shares = jax.random.randint(weight_key, (ROWS, SEGS), 1, 6)
    valid = (SEQ - tails).astype(jnp.int32)
    general = split_lengths(valid, shares)
    half_len = SEQ // 2
    rest_total = jnp.full((ROWS,), SEQ - half_len, jnp.int32)
    rest = split_lengths(rest_total, shares[:, 1:])
    first_row = jnp.concatenate([jnp.full((ROWS, 1), half_len, jnp.int32), rest], axis=1)
    pick_first = (jnp.arange(ROWS) == 0)[:, None]
    return jnp.where(pick_first, first_row, general).astype(jnp.int32)


def levels(own_key, shape, cuts, smallest, high):
    gain = 1.0
    for position, parts in cuts:
        steps = jax.random.uniform(jax.random.fold_in(jax.random.fold_in(own_key, 6), position), (parts,), jnp.float32, smallest / len(cuts), high / len(cuts))
        gain = gain * jnp.repeat(jnp.exp(steps), shape[position] // parts).reshape((-1,) + (1,) * (len(shape) - 1 - position))
    return gain


def noise(own_key, shape, scale, reach, shards=(), kind=jnp.bfloat16):
    result = jax.random.normal(own_key, shape, jnp.float32) * scale
    if len(shards) > 0:
        result = levels(own_key, shape, shards, -0.22, 0.18) * result
    return jnp.clip(result, min=-reach, max=reach).astype(kind)


def setup_inputs(seed: int = 0) -> dict:
    seeds = jax.random.split(jax.random.key(seed), 16)
    tokens = noise(seeds[0], (ROWS, SEQ, D), 1.0, 6.0, ((0, 32),))
    segment_lens = draw_segment_lens(jax.random.fold_in(seeds[15], 71), 0)
    norm1_gain = jnp.clip(1.0 + 0.1 * jax.random.normal(seeds[2], (D,), jnp.float32), 0.5, 1.5)
    norm1_shift = noise(seeds[3], (D,), 0.2, 1.25, (), jnp.float32)
    qkv_weight = noise(seeds[4], (D, HEADS, 3 * HD), D ** -0.5, 0.21875, ((1, 4),))
    qv_bias = noise(seeds[5], (HEADS, 2 * HD), 0.2, 1.25, ((0, 4),), jnp.float32)
    out_weight = noise(seeds[6], (D, D), (D // 32) ** -0.5, 1.25, ((0, 4),))
    out_bias = noise(seeds[7], (D,), 0.2, 1.25, (), jnp.float32)
    norm2_gain = jnp.clip(1.0 + 0.1 * jax.random.normal(seeds[8], (D,), jnp.float32), 0.5, 1.5)
    norm2_shift = noise(seeds[9], (D,), 0.2, 1.25, (), jnp.float32)
    up_weight = noise(seeds[10], (D, FF), D ** -0.5, 0.21875, ((1, 4),))
    up_bias = noise(seeds[11], (FF,), 0.2, 1.25, ((0, 4),), jnp.float32)
    down_weight = noise(seeds[12], (FF, D), FF ** -0.5, 0.109375, ((0, 4),))
    down_bias = noise(seeds[13], (D,), 0.2, 1.25, (), jnp.float32)
    cotangent = noise(seeds[14], (ROWS, SEQ, D), 1.0, 6.0, ((0, 32),))
    return dict(tokens=tokens, segment_lens=segment_lens, norm1_gain=norm1_gain, norm1_shift=norm1_shift, qkv_weight=qkv_weight, qv_bias=qv_bias, out_weight=out_weight, out_bias=out_bias, norm2_gain=norm2_gain, norm2_shift=norm2_shift, up_weight=up_weight, up_bias=up_bias, down_weight=down_weight, down_bias=down_bias, cotangent=cotangent)


@jax.custom_vjp
def low(v):
    return lax.optimization_barrier(v.astype(jnp.bfloat16)).astype(jnp.float32)

@jax.custom_vjp
def low_back(v):
    return v

def low_keep(v):
    return (low(v), None)

def low_pass(kept, grad):
    return (grad,)

def back_keep(v):
    return (v, None)

def back_low(kept, grad):
    return (low(grad),)
low.defvjp(low_keep, low_pass)
low_back.defvjp(back_keep, back_low)
PRECISE = lax.Precision.HIGHEST
EPSILON = 1e-05

def norm_rows(values_in, norm_gain, norm_shift):
    center = values_in - lax.optimization_barrier(jnp.mean(values_in, axis=-1, keepdims=True))
    spread = lax.optimization_barrier(jnp.mean(center * center, axis=-1, keepdims=True))
    return center * lax.rsqrt(spread + EPSILON) * norm_gain + norm_shift

def gelu_exact(activation_in):
    return 0.5 * activation_in * (1.0 + jax.scipy.special.erf(activation_in * 0.7071067811865476))

def doc_numbers(lengths):
    doc_ends = jnp.cumsum(lengths).astype(jnp.int32)
    places = jnp.arange(SEQ, dtype=jnp.int32)
    return lax.optimization_barrier(jnp.sum((places[:, None] >= doc_ends[None, :]).astype(jnp.int32), axis=1))

def allowed_pairs(doc_ids):
    places = jnp.arange(doc_ids.shape[0], dtype=jnp.int32)
    same_doc = (doc_ids[:, None] == doc_ids[None, :]) & (doc_ids[:, None] < SEGS)
    return same_doc | (places[:, None] == places[None, :])

def attend_row(queries, key_rows, value_rows, doc_ids):
    inner_prod = jnp.einsum('qhd,khd->hqk', queries, key_rows, precision=PRECISE)
    scores = low_back(HD ** (-0.5) * inner_prod)
    scores = jnp.where(allowed_pairs(doc_ids)[None], scores, -1e+30)
    row_max = lax.optimization_barrier(jnp.max(scores, axis=-1, keepdims=True))
    expo = jnp.exp(scores - row_max)
    probs = expo / lax.optimization_barrier(jnp.sum(expo, axis=-1, keepdims=True))
    return jnp.einsum('hqk,khd->qhd', low(probs), value_rows, precision=PRECISE)

def attend_item(row_item):
    return jax.checkpoint(attend_row)(row_item[0], row_item[1], row_item[2], row_item[3])

def block_forward(inputs, lengths, norm1_gain, norm1_shift, qkv_weight, qv_bias, out_weight, out_bias, norm2_gain, norm2_shift, up_weight, up_bias, down_weight, down_bias):
    row_count = inputs.shape[0]
    total_rows = row_count * SEQ
    group_heads = HEADS // N_MP
    x_rows = inputs.reshape(total_rows, D)
    normed_one = low(norm_rows(x_rows, norm1_gain, norm1_shift))
    copies_one = low_back(jnp.broadcast_to(normed_one, (N_MP, total_rows, D)))
    qkv_groups = qkv_weight.reshape(D, N_MP, group_heads, 3 * HD)
    projected = jnp.einsum('gtd,dghc->tghc', copies_one, qkv_groups, precision=PRECISE)
    projected = projected.reshape(total_rows, HEADS, 3, HD)
    queries = low(low_back(projected[:, :, 0] + qv_bias[:, :HD]))
    key_rows = low(low_back(projected[:, :, 1]))
    value_rows = low(low_back(projected[:, :, 2] + qv_bias[:, HD:]))
    doc_ids = jax.vmap(doc_numbers)(lengths)
    shape_four = (row_count, SEQ, HEADS, HD)
    context = lax.map(attend_item, (queries.reshape(shape_four), key_rows.reshape(shape_four), value_rows.reshape(shape_four), doc_ids))
    context = low(low_back(context.reshape(total_rows, D)))
    out_groups = out_weight.reshape(N_MP, D // N_MP, D)
    attn_parts = low(jnp.einsum('tgc,gce->tge', context.reshape(total_rows, N_MP, D // N_MP), out_groups, precision=PRECISE))
    attention = low_back(lax.optimization_barrier(jnp.sum(attn_parts, axis=1)) + out_bias)
    resid = x_rows + attention
    normed_two = low(norm_rows(resid, norm2_gain, norm2_shift))
    copies_two = low_back(jnp.broadcast_to(normed_two, (N_MP, total_rows, D)))
    up_groups = up_weight.reshape(D, N_MP, FF // N_MP)
    up_pre = jnp.einsum('gtd,dgf->tgf', copies_two, up_groups, precision=PRECISE) + up_bias.reshape(N_MP, FF // N_MP)
    up_pre = low_back(up_pre)
    hidden = low(gelu_exact(up_pre))
    down_groups = down_weight.reshape(N_MP, FF // N_MP, D)
    ffn_parts = low(jnp.einsum('tgf,gfe->tge', hidden, down_groups, precision=PRECISE))
    mixed = resid + lax.optimization_barrier(jnp.sum(ffn_parts, axis=1)) + down_bias
    return mixed.reshape(row_count, SEQ, D)

def reference(tokens, segment_lens, norm1_gain, norm1_shift, qkv_weight, qv_bias, out_weight, out_bias, norm2_gain, norm2_shift, up_weight, up_bias, down_weight, down_bias, cotangent):
    params = tuple((param.astype(jnp.float32) for param in (norm1_gain, norm1_shift, qkv_weight, qv_bias, out_weight, out_bias, norm2_gain, norm2_shift, up_weight, up_bias, down_weight, down_bias)))
    block_rows = 8
    block_count = ROWS // block_rows
    token_blocks = tokens.reshape(block_count, block_rows, SEQ, D)
    length_blocks = segment_lens.reshape(block_count, block_rows, SEGS)
    cot_blocks = cotangent.reshape(block_count, block_rows, SEQ, D)

    def one_block(running, block_item):
        token_block, length_block, cot_block = block_item

        def forward_fn(inputs, *weights):
            return block_forward(inputs, length_block, *weights)
        mixed_block, pull_back = jax.vjp(forward_fn, token_block.astype(jnp.float32), *params)
        gradients = pull_back(cot_block.astype(jnp.float32))
        running = tuple((running_sum + addend for running_sum, addend in zip(running, gradients[1:])))
        return (running, (mixed_block.astype(jnp.bfloat16), gradients[0]))
    zeros_init = tuple((jnp.zeros(param.shape, jnp.float32) for param in params))
    totals, (mixed, tokens_grad) = lax.scan(one_block, zeros_init, (token_blocks, length_blocks, cot_blocks))
    return (mixed.reshape(ROWS, SEQ, D), tokens_grad.reshape(ROWS, SEQ, D), totals[0], totals[1], totals[2], totals[3], totals[4], totals[5], totals[6], totals[7], totals[8], totals[9], totals[10], totals[11])
```

```python
import jax
import jax.numpy as jnp
from jax import lax
from jax.sharding import Mesh
from jax.sharding import PartitionSpec as P

EPSILON = 1e-05
PLANE = ("z", "x")
DP = ("z", "x", "near")
MP = ("far", "core")
MASKED = -1e30
BF = jnp.bfloat16
F32 = jnp.float32


def norm_parts(values_in):
    center = values_in - jnp.mean(values_in, axis=-1, keepdims=True)
    spread = jnp.mean(center * center, axis=-1, keepdims=True)
    inverse = lax.rsqrt(spread + EPSILON)
    return center * inverse, inverse


def norm_back(grad, xhat, inverse, gain):
    scaled = grad * gain
    centre = jnp.mean(scaled, axis=-1, keepdims=True)
    along = jnp.mean(scaled * xhat, axis=-1, keepdims=True)
    return inverse * (scaled - centre - xhat * along)


def dot(left_side, right_side, left_dim=1, right_dim=0):
    return lax.dot_general(
        left_side, right_side, (((left_dim,), (right_dim,)), ((), ())), preferred_element_type=F32
    )


def shards(
    tokens,
    segment_lens,
    norm1_gain,
    norm1_shift,
    qkv_weight,
    qv_bias,
    out_weight,
    out_bias,
    norm2_gain,
    norm2_shift,
    up_weight,
    up_bias,
    down_weight,
    down_bias,
    cotangent,
):
    row_length, feature_count = tokens.shape[1:]
    heads_here = qkv_weight.shape[1]
    head_size = qkv_weight.shape[2] // 3
    doc_count = segment_lens.shape[1]
    score_scale = head_size ** (-0.5)
    half = row_length // 2
    plane_count = lax.axis_size(PLANE)
    core = lax.axis_index("core")
    mine_at, other_at = core * half, (1 - core) * half

    def core_swap(array_in):
        return lax.ppermute(array_in, "core", [(0, 1), (1, 0)])

    def chip_swap(array_in):
        return lax.ppermute(array_in, "far", [(0, 1), (1, 0)])

    def near_swap(array_in):
        return lax.ppermute(array_in, "near", [(0, 1), (1, 0)])

    def own_first(array_in):
        return jnp.concatenate(
            (
                lax.dynamic_slice_in_dim(array_in, mine_at, half),
                lax.dynamic_slice_in_dim(array_in, other_at, half),
            )
        )

    def in_order(mine, other):
        first = core == 0
        return jnp.concatenate((jnp.where(first, mine, other), jnp.where(first, other, mine)))

    def sum_half(part):
        received = core_swap(part[half:].astype(BF))
        pair = (part[:half] + received.astype(F32)).astype(BF)
        return pair.astype(F32) + chip_swap(pair).astype(F32)

    def both_halves(mine):
        return jnp.concatenate((mine, core_swap(mine)))

    def scatter(grads):
        chunks = [g.astype(BF).reshape(plane_count, -1, feature_count) for g in grads]
        return lax.all_to_all(jnp.concatenate(chunks, axis=1), PLANE, 0, 0, tiled=True)

    def finish(received):
        pair = jnp.sum(received.astype(F32), axis=0).astype(BF)
        return (pair.astype(F32) + near_swap(pair).astype(F32)).astype(BF)

    def gather(chunk):
        copies = jnp.broadcast_to(chunk[None], (plane_count,) + chunk.shape)
        return lax.all_to_all(copies, PLANE, 0, 0, tiled=True)

    x_rows = own_first(tokens[0]).astype(F32)
    cot_rows = own_first(cotangent[0])
    xhat_one, inverse_one = norm_parts(x_rows)
    normed_one = (xhat_one * norm1_gain + norm1_shift).astype(BF)
    qkv_rows = qkv_weight.transpose(1, 2, 0).reshape(heads_here * 3 * head_size, feature_count)
    projected = dot(normed_one, qkv_rows, 1, 1).reshape(row_length, heads_here, 3, head_size)
    queries = (projected[:, :, 0] + qv_bias[None, :, :head_size]).astype(BF)
    key_rows = projected[:, :, 1].astype(BF)
    value_rows = (projected[:, :, 2] + qv_bias[None, :, head_size:]).astype(BF)

    doc_ends = jnp.cumsum(segment_lens[0])
    places = own_first(jnp.arange(row_length, dtype=jnp.int32))
    doc_ids = jnp.sum((places[:, None] >= doc_ends[None, :]).astype(jnp.int32), axis=1)
    same_doc = (doc_ids[:, None] == doc_ids[None, :]) & (doc_ids[:, None] < doc_count)
    allowed = same_doc | (places[:, None] == places[None, :])

    scores = jnp.einsum("qhd,khd->hqk", queries, key_rows, preferred_element_type=F32) * score_scale
    scores = jnp.where(allowed[None], scores, MASKED)
    row_max = jnp.max(scores, axis=-1, keepdims=True)
    expo = jnp.exp(scores - row_max)
    row_total = jnp.sum(expo, axis=-1, keepdims=True)
    probs = expo / row_total
    probs_low = probs.astype(BF)
    context = jnp.einsum("hqk,khd->qhd", probs_low, value_rows, preferred_element_type=F32)
    context = context.astype(BF).reshape(row_length, heads_here * head_size)

    resid = x_rows[:half] + sum_half(dot(context, out_weight)) + out_bias
    xhat_two, inverse_two = norm_parts(resid)
    normed_two = both_halves((xhat_two * norm2_gain + norm2_shift).astype(BF))
    up_pre = dot(normed_two, up_weight) + up_bias
    cumulative = 0.5 * (1.0 + lax.erf(up_pre * 0.7071067811865476))
    hidden = (up_pre * cumulative).astype(BF)
    slope = cumulative + up_pre * (jnp.exp(-0.5 * up_pre * up_pre) * 0.3989422804014327)
    up_grad = (dot(cot_rows, down_weight, 1, 1) * slope).astype(BF)

    normed_two_grad = sum_half(dot(up_grad, up_weight, 1, 1))
    resid_grad = cot_rows[:half].astype(F32) + norm_back(
        normed_two_grad, xhat_two, inverse_two, norm2_gain
    )
    attention_grad_half = resid_grad.astype(BF)
    attention_grad = both_halves(attention_grad_half)

    expert_parts = scatter((dot(hidden, cot_rows, 0, 0), dot(normed_two, up_grad, 0, 0)))

    mixed_half = (resid + sum_half(dot(hidden, down_weight)) + down_bias).astype(BF)
    mixed = in_order(mixed_half, core_swap(mixed_half))

    context_grad = dot(attention_grad, out_weight, 1, 1).astype(BF)
    context_grad = context_grad.reshape(row_length, heads_here, head_size)
    probs_grad = jnp.einsum("qhd,khd->hqk", context_grad, value_rows, preferred_element_type=F32)
    value_grad = jnp.einsum("hqk,qhd->khd", probs_low, context_grad, preferred_element_type=F32)
    centre = jnp.sum(probs_grad * probs, axis=-1, keepdims=True)
    score_grad = (probs * (probs_grad - centre)).astype(BF)
    query_grad = jnp.einsum("hqk,khd->qhd", score_grad, key_rows, preferred_element_type=F32)
    key_grad = jnp.einsum("hqk,qhd->khd", score_grad, queries, preferred_element_type=F32)
    query_grad = (query_grad * score_scale).astype(BF)
    key_grad = (key_grad * score_scale).astype(BF)
    value_grad = value_grad.astype(BF)
    qkv_grad = jnp.stack((query_grad, key_grad, value_grad), axis=2).reshape(row_length, -1)

    normed_one_grad = sum_half(dot(qkv_grad, qkv_rows))
    xhat_half = xhat_one[:half]
    tokens_grad_half = resid_grad + norm_back(
        normed_one_grad, xhat_half, inverse_one[:half], norm1_gain
    )
    tokens_grad = in_order(tokens_grad_half, core_swap(tokens_grad_half))

    attend_parts = scatter(
        (
            dot(qkv_grad, normed_one, 0, 0),
            dot(context, attention_grad, 0, 0),
        )
    )
    expert_sum = finish(expert_parts)
    expert_sum, attend_parts = lax.optimization_barrier((expert_sum, attend_parts))
    expert_grads = gather(expert_sum)
    attend_sum = finish(attend_parts)

    halves = jnp.stack(
        (
            jnp.sum(normed_one_grad * xhat_half, axis=0),
            jnp.sum(normed_one_grad, axis=0),
            jnp.sum(normed_two_grad * xhat_two, axis=0),
            jnp.sum(normed_two_grad, axis=0),
            jnp.sum(attention_grad_half.astype(F32), axis=0),
            jnp.sum(cot_rows[:half].astype(F32), axis=0),
        )
    )
    halves = halves + core_swap(halves)
    qv_sums = jnp.stack((query_grad, value_grad), axis=2).astype(F32).sum(axis=0).reshape(-1)
    whole = jnp.stack(
        (
            jnp.sum(up_grad.astype(F32), axis=0),
            jnp.pad(qv_sums, (0, feature_count - qv_sums.shape[0])),
        )
    )
    vectors = jnp.concatenate((halves, whole))
    vectors = (vectors + near_swap(vectors)).astype(BF)

    expert_grads, attend_sum = lax.optimization_barrier((expert_grads, attend_sum))
    last = gather(jnp.concatenate((attend_sum, vectors)))
    chunk_rows = attend_sum.shape[0]
    expert_grads = expert_grads.astype(F32)
    attend_grads = last[:, :chunk_rows].astype(F32)
    vector_sums = jnp.sum(last[:, chunk_rows:].astype(F32), axis=0)

    def rows_of(grads, first, count):
        return grads[:, first : first + count].reshape(-1, feature_count)

    qkv_chunk = heads_here * 3 * head_size // plane_count
    down_chunk = hidden.shape[1] // plane_count
    qkv_weight_grad = rows_of(attend_grads, 0, qkv_chunk).reshape(
        heads_here, 3 * head_size, feature_count
    )
    return (
        mixed[None],
        tokens_grad[None],
        vector_sums[0],
        vector_sums[1],
        qkv_weight_grad.transpose(2, 0, 1),
        vector_sums[7, : qv_sums.shape[0]].reshape(heads_here, 2 * head_size),
        rows_of(attend_grads, qkv_chunk, chunk_rows - qkv_chunk),
        vector_sums[4],
        vector_sums[2],
        vector_sums[3],
        rows_of(expert_grads, down_chunk, feature_count // plane_count),
        vector_sums[6],
        rows_of(expert_grads, 0, down_chunk),
        vector_sums[5],
    )


def solution(mesh):
    fine = Mesh(mesh.devices.reshape(4, 4, 2, 2, 2), ("z", "x", "near", "far", "core"))
    rows, heads, features = P(DP, None, None), P(MP, None), P(MP)
    placed = (
        rows,
        P(DP, None),
        P(),
        P(),
        P(None, MP, None),
        heads,
        heads,
        P(),
        P(),
        P(),
        P(None, MP),
        features,
        heads,
        P(),
        rows,
    )
    given = (
        rows,
        rows,
        P(),
        P(),
        P(None, MP, None),
        heads,
        heads,
        P(),
        P(),
        P(),
        P(None, MP),
        features,
        heads,
        P(),
    )
    return jax.shard_map(shards, mesh=fine, in_specs=placed, out_specs=given, check_vma=False)
```

```python
import jax
import jax.numpy as jnp
from jax import lax
from jax.experimental import pallas as pl
from jax.experimental.pallas import tpu as pltpu
from jax.sharding import Mesh
from jax.sharding import PartitionSpec as P

EPSILON = 1e-05
MASKED = -1e30
BF = jnp.bfloat16
F32 = jnp.float32
PLANE = ("z", "x")
DP = ("z", "x", "near")
MP = ("far", "core")
SMEM = pltpu.SMEM


def dot(left_side, right_side, left_dim=1, right_dim=0):
    return lax.dot_general(
        left_side, right_side, (((left_dim,), (right_dim,)), ((), ())), preferred_element_type=F32
    )


def call(body, outs, scratch=(), place=pltpu.VMEM, limit=12 << 20, cost=1000):
    def run(*arrays):
        space = pl.BlockSpec() if place is None else pl.BlockSpec(memory_space=place)
        return pl.pallas_call(
            body,
            out_shape=[jax.ShapeDtypeStruct(s, d) for s, d in outs],
            in_specs=[space] * len(arrays),
            out_specs=[space] * len(outs),
            scratch_shapes=[pltpu.VMEM(*s) if isinstance(s, tuple) else s for s in scratch],
            cost_estimate=pl.CostEstimate(flops=cost, bytes_accessed=1000, transcendentals=0),
            compiler_params=pltpu.CompilerParams(vmem_limit_bytes=limit),
            name=body.__name__,
        )(*arrays)

    return run


def line(ref):
    return ref[...].reshape(1, -1)


def norm_parts(values_in):
    center = values_in - jnp.mean(values_in, axis=-1, keepdims=True)
    spread = jnp.mean(center * center, axis=-1, keepdims=True)
    inverse = lax.rsqrt(spread + EPSILON)
    return center * inverse, inverse


def norm_back(grad, xhat, inverse, gain):
    scaled = grad * gain
    centre = jnp.mean(scaled, axis=-1, keepdims=True)
    along = jnp.mean(scaled * xhat, axis=-1, keepdims=True)
    return inverse * (scaled - centre - xhat * along)


def half_at(which, half):
    core = lax.axis_index("core")
    return pl.multiple_of((core if which == 0 else 1 - core) * half, half)


def fold(rows):
    return jnp.sum(rows, axis=0, keepdims=True)


def attend_kernel(
    lens_ref,
    tok_ref,
    gain_ref,
    shift_ref,
    w_ref,
    bias_ref,
    out_ref,
    normed_out,
    qkv_out,
    probs_out,
    ctx_out,
    own_out,
    other_out,
    normed_ref,
    qkv_ref,
    probs_ref,
    ctx_ref,
    own_ref,
    other_ref,
    lens_at,
    tok_at,
    gain_at,
    shift_at,
    w_at,
    bias_at,
    out_at,
    semaphores,
):
    length, features = tok_ref.shape
    half = length // 2
    heads = bias_ref.shape[0]
    size = bias_ref.shape[1] // 2
    copies = []

    def fetch(source, target):
        copies.append(pltpu.make_async_copy(source, target, semaphores.at[len(copies)]))
        copies[-1].start()
        return copies[-1]

    piece = half // 2
    pieces = []
    for which in range(2):
        for part in range(2):
            start = half_at(which, half) + part * piece
            at = which * half + part * piece
            pieces.append(fetch(tok_ref.at[pl.ds(start, piece)], tok_at.at[pl.ds(at, piece)]))
    norms = [fetch(gain_ref, gain_at), fetch(shift_ref, shift_at)]
    weights = []
    for head in range(heads):
        rows = pl.ds(head * 3 * size, 3 * size)
        weights.append(fetch(w_ref.at[rows], w_at.at[rows]))
    bias_copy, lens_copy = fetch(bias_ref, bias_at), fetch(lens_ref, lens_at)
    out_copy = fetch(out_ref, out_at)
    for copy in norms:
        copy.wait()
    step = 64
    for index, copy in enumerate(pieces):
        copy.wait()
        for first in range(index * piece, (index + 1) * piece, step):
            xhat, _ = norm_parts(tok_at[first : first + step, :].astype(F32))
            normed_ref[first : first + step, :] = (xhat * line(gain_at) + line(shift_at)).astype(BF)
    leaving = [fetch(normed_ref, normed_out)]
    bias_copy.wait()
    lens_copy.wait()
    lens_ref, bias_ref, w_ref = lens_at, bias_at, w_at

    diagonal = lax.broadcasted_iota(jnp.int32, (2 * size, 2 * size), 0) == (
        lax.broadcasted_iota(jnp.int32, (2 * size, 2 * size), 1)
    )
    for head in range(heads):
        base = head * 3 * size
        column = jnp.sum(
            jnp.where(diagonal, bias_ref[head : head + 1, :], 0.0), axis=1, keepdims=True
        )
        weights[head].wait()
        projected = dot(w_ref[base : base + 3 * size, :], normed_ref[...], 1, 1)
        qkv_ref[base : base + size, :] = (projected[:size] + column[:size]).astype(BF)
        qkv_ref[base + size : base + 2 * size, :] = projected[size : 2 * size].astype(BF)
        qkv_ref[base + 2 * size : base + 3 * size, :] = (
            projected[2 * size :] + column[size:]
        ).astype(BF)
    leaving.append(fetch(qkv_ref, qkv_out))

    docs = lens_ref.shape[1]
    ends = [lens_ref[0, 0]]
    for doc in range(1, docs):
        ends.append(ends[-1] + lens_ref[0, doc])

    def numbers(shape, dim, first):
        place = lax.broadcasted_iota(jnp.int32, shape, dim) + first + lax.axis_index("core") * half
        place = jnp.where(place >= length, place - length, place)
        number = jnp.zeros(shape, jnp.int32)
        for end in ends:
            number += (place >= end).astype(jnp.int32)
        return jnp.where(number >= docs, docs + place, number)

    key_docs = numbers((1, length), 1, 0)
    block = 128
    query_docs = [numbers((block, 1), 0, first) for first in range(0, length, block)]
    scale = size ** (-0.5)
    for head in range(heads):
        base = head * 3 * size
        keys = qkv_ref[base + size : base + 2 * size, :]
        for index in range(length // block):
            rows = slice(index * block, (index + 1) * block)
            scores = dot(qkv_ref[base : base + size, rows], keys, 0, 0) * scale
            scores = jnp.where(query_docs[index] == key_docs, scores, MASKED)
            expo = jnp.exp(scores - jnp.max(scores, axis=-1, keepdims=True))
            probs = expo * (1.0 / jnp.sum(expo, axis=-1, keepdims=True))
            probs_ref[head, rows, :] = probs.astype(BF)
        leaving.append(fetch(probs_ref.at[head], probs_out.at[head]))
        values = qkv_ref[base + 2 * size : base + 3 * size, :]
        ctx_ref[head * size : (head + 1) * size, :] = dot(values, probs_ref[head], 1, 1).astype(BF)
    leaving.append(fetch(ctx_ref, ctx_out))
    out_copy.wait()
    other_ref[...] = dot(ctx_ref[:, half:], out_at[...], 0, 0).astype(BF)
    leaving.append(fetch(other_ref, other_out))
    own_ref[...] = dot(ctx_ref[:, :half], out_at[...], 0, 0)
    leaving.append(fetch(own_ref, own_out))
    for copy in leaving:
        copy.wait()


def resid_kernel(tok_ref, pair_ref, come_ref, bias_ref, gain_ref, shift_ref, normed_ref, resid_ref):
    half = pair_ref.shape[0]
    start = half_at(0, half)
    step = 64
    for first in range(0, half, step):
        rows = slice(first, first + step)
        resid = (
            tok_ref[pl.ds(start + first, step), :].astype(F32)
            + (pair_ref[rows, :].astype(F32) + come_ref[rows, :].astype(F32))
            + line(bias_ref)
        )
        resid_ref[rows, :] = resid
        xhat, _ = norm_parts(resid)
        normed_ref[rows, :] = (xhat * line(gain_ref) + line(shift_ref)).astype(BF)


def expert_kernel(
    mine_ref,
    theirs_ref,
    up_ref,
    bias_ref,
    down_ref,
    cot_ref,
    hidden_ref,
    grad_ref,
    own_ref,
    other_ref,
    sum_ref,
):
    half = mine_ref.shape[0]
    step = 128
    total = jnp.zeros((1, up_ref.shape[1]), F32)
    for which in (1, 0):
        start = half_at(which, half)
        for first in range(0, half, step):
            rows = slice(first, first + step)
            normed = (theirs_ref if which else mine_ref)[rows, :]
            pre = dot(normed, up_ref[...]) + line(bias_ref)
            back = dot(cot_ref[pl.ds(start + first, step), :], down_ref[...], 1, 1)
            cumulative = 0.5 * (1.0 + lax.erf(pre * 0.7071067811865476))
            at = slice(which * half + first, which * half + first + step)
            hidden_ref[at, :] = (pre * cumulative).astype(BF)
            slope = cumulative + pre * (jnp.exp(-0.5 * pre * pre) * 0.3989422804014327)
            grad = (back * slope).astype(BF)
            grad_ref[at, :] = grad
            total += fold(grad.astype(F32))
            part = dot(grad, up_ref[...], 1, 1)
            if which:
                other_ref[rows, :] = part.astype(BF)
            else:
                own_ref[rows, :] = part
    sum_ref[...] = total


def expert_weights_kernel(hidden_ref, cot_ref, mine_ref, theirs_ref, grad_ref, chunk_ref):
    half = mine_ref.shape[0]
    count, pair, _ = chunk_ref.shape
    each = pair // 2
    cot_mine = cot_ref[pl.ds(half_at(0, half), half), :]
    cot_theirs = cot_ref[pl.ds(half_at(1, half), half), :]
    some = 4
    for first in range(0, count, some):
        columns = slice(first * each, (first + some) * each)
        down = dot(hidden_ref[:half, columns], cot_mine, 0, 0)
        down += dot(hidden_ref[half:, columns], cot_theirs, 0, 0)
        chunk_ref[first : first + some, :each, :] = down.astype(BF).reshape(some, each, -1)
        up = dot(mine_ref[:, columns], grad_ref[:half, :], 0, 0)
        up += dot(theirs_ref[:, columns], grad_ref[half:, :], 0, 0)
        chunk_ref[first : first + some, each:, :] = up.astype(BF).reshape(some, each, -1)


def second_norm_kernel(
    pair_ref, come_ref, resid_ref, gain_ref, cot_ref, low_ref, grad_ref, rows_ref
):
    half = resid_ref.shape[0]
    start = half_at(0, half)
    step = 64
    gains, shifts, outs, downs = 0.0, 0.0, 0.0, 0.0
    for first in range(0, half, step):
        rows = slice(first, first + step)
        xhat, inverse = norm_parts(resid_ref[rows, :])
        grad = pair_ref[rows, :].astype(F32) + come_ref[rows, :].astype(F32)
        cot = cot_ref[pl.ds(start + first, step), :].astype(F32)
        back = cot + norm_back(grad, xhat, inverse, line(gain_ref))
        grad_ref[rows, :] = back
        low = back.astype(BF)
        low_ref[rows, :] = low
        gains += fold(grad * xhat)
        shifts += fold(grad)
        outs += fold(low.astype(F32))
        downs += fold(cot)
    rows_ref[...] = jnp.zeros_like(rows_ref)
    for index, value in ((2, gains), (3, shifts), (4, outs), (5, downs)):
        rows_ref[index : index + 1, :] = value


def attend_back_kernel(
    mine_ref,
    theirs_ref,
    out_ref,
    probs_ref,
    qkv_ref,
    ctx_ref,
    normed_ref,
    grads_ref,
    chunk_ref,
    sums_ref,
    back_ref,
    score_ref,
):
    heads, length, _ = probs_ref.shape
    half = length // 2
    size = ctx_ref.shape[0] // heads
    scale = size ** (-0.5)
    back_ref[:, :half] = dot(out_ref[...], mine_ref[...], 1, 1).astype(BF)
    back_ref[:, half:] = dot(out_ref[...], theirs_ref[...], 1, 1).astype(BF)
    block = 128
    for head in range(heads):
        base = head * 3 * size
        own = slice(head * size, (head + 1) * size)
        queries = qkv_ref[base : base + size, :]
        keys = qkv_ref[base + size : base + 2 * size, :]
        values = qkv_ref[base + 2 * size : base + 3 * size, :]
        for first in range(0, length, block):
            rows = slice(first, first + block)
            probs = probs_ref[head, rows, :].astype(F32)
            probs_grad = dot(back_ref[own, rows], values, 0, 0)
            centre = jnp.sum(probs_grad * probs, axis=-1, keepdims=True)
            score_ref[rows, :] = (probs * (probs_grad - centre)).astype(BF)
        score_grad = score_ref[...]
        grads_ref[base : base + size, :] = (dot(keys, score_grad, 1, 1) * scale).astype(BF)
        grads_ref[base + size : base + 2 * size, :] = (dot(queries, score_grad) * scale).astype(BF)
        grads_ref[base + 2 * size : base + 3 * size, :] = dot(
            back_ref[own, :], probs_ref[head]
        ).astype(BF)
    width = grads_ref.shape[0]
    each = chunk_ref.shape[1]
    some = 4
    for first in range(0, width, some * each):
        grad = dot(grads_ref[first : first + some * each, :], normed_ref[...]).astype(BF)
        at = first // each
        chunk_ref[at : at + some] = grad.reshape(some, each, -1)
    outs = dot(ctx_ref[:, :half], mine_ref[...]) + dot(ctx_ref[:, half:], theirs_ref[...])
    chunk_ref[width // each :] = outs.astype(BF).reshape(-1, each, outs.shape[1])
    sums_ref[...] = dot(jnp.ones((8, length), BF), grads_ref[...], 1, 1)


def parts_kernel(grads_ref, w_ref, hidden_ref, down_ref, own_ref, other_ref):
    half = own_ref.shape[0] // 2
    other_ref[:half, :] = dot(grads_ref[:, half:], w_ref[...], 0, 0).astype(BF)
    other_ref[half:, :] = dot(hidden_ref[half:, :], down_ref[...]).astype(BF)
    own_ref[:half, :] = dot(grads_ref[:, :half], w_ref[...], 0, 0)
    own_ref[half:, :] = dot(hidden_ref[:half, :], down_ref[...])


def first_norm_kernel(
    tok_ref, pair_ref, come_ref, gain_ref, bias_ref, back_ref, resid_ref, rows_ref, grad_ref, mixed_ref
):
    half = mixed_ref.shape[0]
    start = half_at(0, half)
    step = 64
    gains, shifts = 0.0, 0.0
    for first in range(0, half, step):
        rows = slice(first, first + step)
        below = slice(half + first, half + first + step)
        xhat, inverse = norm_parts(tok_ref[pl.ds(start + first, step), :].astype(F32))
        grad = pair_ref[rows, :].astype(F32) + come_ref[rows, :].astype(F32)
        grad_ref[rows, :] = back_ref[rows, :] + norm_back(grad, xhat, inverse, line(gain_ref))
        out = pair_ref[below, :].astype(F32) + come_ref[below, :].astype(F32)
        mixed_ref[rows, :] = (resid_ref[rows, :] + out + line(bias_ref)).astype(BF)
        gains += fold(grad * xhat)
        shifts += fold(grad)
    grad_ref[half:, :] = rows_ref[...]
    grad_ref[half : half + 1, :] = gains
    grad_ref[half + 1 : half + 2, :] = shifts


def mixed_order_kernel(mine_ref, theirs_ref, row_ref):
    half = mine_ref.shape[0]
    row_ref[pl.ds(half_at(0, half), half), :] = mine_ref[...]
    row_ref[pl.ds(half_at(1, half), half), :] = theirs_ref[...]


def token_order_kernel(mine_ref, theirs_ref, up_ref, qkv_ref, row_ref, whole_ref):
    half = row_ref.shape[0] // 2
    row_ref[pl.ds(half_at(0, half), half), :] = mine_ref[:half, :]
    row_ref[pl.ds(half_at(1, half), half), :] = theirs_ref[:half, :]
    whole_ref[...] = mine_ref[half:, :] + theirs_ref[half:, :]
    whole_ref[6:7, :] = up_ref[...]
    whole_ref[7:8, : qkv_ref.shape[1]] = qkv_ref[0:1, :]


def pair_kernel(own_ref, come_ref, pair_ref):
    pair_ref[...] = (own_ref[...] + come_ref[...].astype(F32)).astype(BF)


def expert_finish_kernel(pair_ref, come_ref, a_ref, b_ref):
    split = a_ref.shape[0]
    a_ref[...] = pair_ref[:split, :] + come_ref[:split, :]
    b_ref[...] = pair_ref[split:, :] + come_ref[split:, :]


def total_kernel(parts_ref, total_ref):
    step = 16
    for first in range(0, total_ref.shape[0], step):
        rows = slice(first, first + step)
        total = parts_ref[0, rows, :].astype(F32)
        for part in range(1, parts_ref.shape[0]):
            total += parts_ref[part, rows, :].astype(F32)
        total_ref[rows, :] = total.astype(BF)


def attend_total_kernel(parts_ref, whole_ref, pair_ref):
    count = parts_ref.shape[1]
    total_kernel(parts_ref, pair_ref.at[:count])
    vectors = whole_ref[...]
    pair_ref[count:, :] = jnp.concatenate((vectors, jnp.zeros_like(vectors))).astype(BF)


def attend_finish_kernel(pair_ref, come_ref, total_ref):
    total_ref[...] = pair_ref[...] + come_ref[...]


def place(axis, blocks, store):
    count = len(blocks)
    for shift, block in enumerate(blocks):
        store(lax.rem(lax.axis_index(axis) + count - shift, count), block)


def expert_small_kernel(*refs):
    a_blocks, b_blocks, (a_ref, b_ref) = refs[:4], refs[4:8], refs[8:]
    each = a_blocks[0].shape[0]

    def store_a(source, block):
        for copy in range(a_ref.shape[0]):
            a_ref[copy, pl.ds(pl.multiple_of(source * each, each), each), :] = block[...]

    def store_b(source, block):
        b_ref[pl.ds(pl.multiple_of(source * each, each), each), :] = block[...]

    place("z", a_blocks, store_a)
    place("x", b_blocks, store_b)


def expert_last_kernel(parts_ref, *refs):
    blocks, (down_ref, up_ref) = refs[:4], refs[4:]
    planes = parts_ref.shape[0]
    rows = blocks[0].shape[0]
    each = rows // planes
    for x in range(planes):
        for z in range(planes):
            at = (z * planes + x) * each
            down_ref[at : at + each, :] = parts_ref[x, z * each : (z + 1) * each, :].astype(F32)

    def store(source, block):
        up_ref[pl.ds(pl.multiple_of(source * rows, rows), rows), :] = block[...].astype(F32)

    place("z", blocks, store)


def attend_small_kernel(*refs):
    blocks, (copies_ref, keep_ref) = refs[:4], refs[4:]
    each = blocks[0].shape[0] - keep_ref.shape[1]
    planes = keep_ref.shape[0]

    def store(source, block):
        keep_ref[source] = block[each:, :].astype(F32)
        for copy in range(planes):
            copies_ref[copy, pl.ds(pl.multiple_of(source * each, each), each), :] = block[:each, :]

    place("z", blocks, store)
    total = keep_ref[0]
    for source in range(1, planes):
        total += keep_ref[source]
    for copy in range(planes):
        copies_ref[copy, planes * each :, :] = total.astype(BF)


def attend_last_kernel(parts_ref, qkv_ref, out_ref, qv_ref, *vector_refs):
    planes = parts_ref.shape[0]
    each = (parts_ref.shape[1] - 16) // planes
    width = qkv_ref.shape[0]
    for x in range(planes):
        for z in range(planes):
            rows = parts_ref[x, z * each : (z + 1) * each, :].astype(F32)
            at = (z * planes + x) * each
            if at < width:
                qkv_ref[at : at + each, :] = rows
            else:
                out_ref[at - width : at - width + each, :] = rows
    total = parts_ref[0, planes * each :, :].astype(F32)
    for x in range(1, planes):
        total += parts_ref[x, planes * each :, :].astype(F32)
    for index, vector_ref in enumerate(vector_refs):
        vector_ref[...] = total[index]
    heads, double = qv_ref.shape
    size = double // 2
    for head in range(heads):
        base = 3 * head * size
        qv_ref[head : head + 1, :size] = total[7:8, base : base + size]
        qv_ref[head : head + 1, size:] = total[7:8, base + 2 * size : base + 3 * size]


def shards(
    tokens,
    segment_lens,
    norm1_gain,
    norm1_shift,
    qkv_weight,
    qv_bias,
    out_weight,
    out_bias,
    norm2_gain,
    norm2_shift,
    up_weight,
    up_bias,
    down_weight,
    down_bias,
    cotangent,
):
    length, features = tokens.shape[1:]
    heads = qkv_weight.shape[1]
    size = qkv_weight.shape[2] // 3
    width = heads * 3 * size
    units = up_weight.shape[1]
    half = length // 2
    plane = lax.axis_size(PLANE)
    side = lax.axis_size("x")
    tok, cot = tokens[0], cotangent[0]
    qkv_rows = qkv_weight.transpose(1, 2, 0).reshape(width, features)

    def core_swap(array_in):
        return lax.ppermute(array_in, "core", [(0, 1), (1, 0)])

    def chip_swap(array_in):
        return lax.ppermute(array_in, "far", [(0, 1), (1, 0)])

    def near_swap(array_in):
        return lax.ppermute(array_in, "near", [(0, 1), (1, 0)])

    def add_pair(own, other):
        return call(pair_kernel, ((other.shape, BF),))(own, core_swap(other))[0]

    def scatter(chunks):
        return lax.all_to_all(chunks, PLANE, 0, 0, tiled=True)

    def plane_sum(received):
        return call(total_kernel, ((received.shape[1:], BF),))(received)[0]

    def along(block, axis):
        moves = [[(i, (i + shift) % side) for i in range(side)] for shift in range(1, side)]
        far, near, back = (lax.ppermute(block, axis, moves[i]) for i in (1, 0, 2))
        return (block, near, far, back)

    def spread(copies):
        return lax.all_to_all(copies, "x", 0, 0, tiled=True)

    half_low, half_full = ((half, features), BF), ((half, features), F32)
    row_low, row_full = ((length, features), BF), ((length, features), F32)
    rows_full = ((8, features), F32)
    count = heads * size

    outs = (
        row_low,
        ((width, length), BF),
        ((heads, length, length), BF),
        ((count, length), BF),
        half_full,
        half_low,
    )
    staged = (
        pltpu.SMEM(segment_lens.shape, segment_lens.dtype),
        row_low,
        ((features,), F32),
        ((features,), F32),
        ((width, features), BF),
        (qv_bias.shape, F32),
        (out_weight.shape, BF),
        pltpu.SemaphoreType.DMA((14 + 2 * heads,)),
    )
    normed_one, qkv, probs, context, own, other = call(
        attend_kernel, outs, outs + staged, pltpu.HBM, 60 << 20
    )(segment_lens, tok, norm1_gain, norm1_shift, qkv_rows, qv_bias, out_weight)
    pair = add_pair(own, other)
    normed_mine, resid = call(resid_kernel, (half_low, half_full))(
        tok, pair, chip_swap(pair), out_bias, norm2_gain, norm2_shift
    )
    normed_theirs = core_swap(normed_mine)

    hidden, up_grad, own, other, up_sums = call(
        expert_kernel,
        (((length, units), BF), ((length, units), BF), half_full, half_low, ((1, units), F32)),
    )(normed_mine, normed_theirs, up_weight, up_bias, down_weight, cot)
    pair = add_pair(own, other)
    pair, hidden = lax.optimization_barrier((pair, hidden))
    (chunks,) = call(
        expert_weights_kernel,
        (((plane, (units + features) // plane, features), BF),),
        cost=20_000_000_000,
    )(hidden, cot, normed_mine, normed_theirs, up_grad)
    come = chip_swap(pair)
    expert_parts = scatter(chunks)
    low_mine, resid_grad, sums = call(second_norm_kernel, (half_low, half_full, rows_full))(
        pair, come, resid, norm2_gain, cot
    )
    low_theirs = core_swap(low_mine)

    qkv_grad, chunks, qkv_sums = call(
        attend_back_kernel,
        (((width, length), BF), ((plane, (width + count) // plane, features), BF), ((8, width), F32)),
        (((count, length), BF), ((length, length), BF)),
    )(low_mine, low_theirs, out_weight, probs, qkv, context, normed_one)
    attend_parts = scatter(chunks)
    own, other = call(parts_kernel, (row_full, row_low))(qkv_grad, qkv_rows, hidden, down_weight)
    parts_pair = add_pair(own, other)

    pair = plane_sum(expert_parts)
    each = pair.shape[0] // 2
    come = near_swap(pair)
    come, parts_pair = lax.optimization_barrier((come, parts_pair))
    blocks = call(expert_finish_kernel, (((each, features), BF),) * 2)(pair, come)
    copies, block = call(
        expert_small_kernel,
        (((side, side * each, features), BF), ((side * each, features), BF)),
    )(*along(blocks[0], "z"), *along(blocks[1], "x"))
    copies, attend_parts = lax.optimization_barrier((copies, attend_parts))
    come, _ = lax.optimization_barrier((chip_swap(parts_pair), block))
    gathered = spread(copies)
    expert_blocks = along(block, "z")

    token_grad, mixed = call(first_norm_kernel, (((half + 8, features), F32), half_low))(
        tok, parts_pair, come, norm1_gain, down_bias, resid_grad, resid, sums
    )
    tokens_grad, whole = call(token_order_kernel, (row_full, rows_full))(
        token_grad, core_swap(token_grad), up_sums, qkv_sums
    )
    (mixed,) = call(mixed_order_kernel, (row_low,))(mixed, core_swap(mixed))

    rows = attend_parts.shape[1] + 16
    (pair,) = call(attend_total_kernel, (((rows, features), BF),))(attend_parts, whole)
    (block,) = call(attend_finish_kernel, (((rows, features), BF),))(pair, near_swap(pair))
    blocks, expert_blocks = lax.optimization_barrier((along(block, "z"), expert_blocks))
    (copies,) = call(
        attend_small_kernel,
        (((side, side * (rows - 16) + 16, features), BF),),
        (((side, 16, features), F32),),
    )(*blocks)
    copies, gathered = lax.optimization_barrier((copies, gathered))
    down_grad, up_weight_grad = call(
        expert_last_kernel,
        (((units, features), F32), ((features, units), F32)),
        place=None,
        limit=60 << 20,
    )(gathered, *expert_blocks)
    qkv_grads, out_weight_grad, qv_bias_grad, *vectors = call(
        attend_last_kernel,
        (((width, features), F32), ((count, features), F32), (qv_bias.shape, F32))
        + (((features,), F32),) * 7,
    )(spread(copies))
    return (
        mixed[None],
        tokens_grad[None],
        vectors[0],
        vectors[1],
        qkv_grads.reshape(heads, 3 * size, features).transpose(2, 0, 1),
        qv_bias_grad,
        out_weight_grad,
        vectors[4],
        vectors[2],
        vectors[3],
        up_weight_grad,
        vectors[6],
        down_grad,
        vectors[5],
    )


def solution(mesh):
    fine = Mesh(mesh.devices.reshape(4, 4, 2, 2, 2), ("z", "x", "near", "far", "core"))
    rows, first, features = P(DP, None, None), P(MP, None), P(MP)
    weights = (
        P(),
        P(),
        P(None, MP, None),
        first,
        first,
        P(),
        P(),
        P(),
        P(None, MP),
        features,
        first,
        P(),
    )
    return jax.shard_map(
        shards,
        mesh=fine,
        in_specs=(rows, P(DP, None)) + weights + (rows,),
        out_specs=(rows, rows) + weights,
        check_vma=False,
    )
```

```python
import jax
import jax.numpy as jnp
from jax import lax
from jax.experimental import pallas as pl
from jax.experimental.pallas import tpu as pltpu
from jax.sharding import Mesh
from jax.sharding import PartitionSpec as P

EPSILON = 1e-05
MASKED = -1e30
BF = jnp.bfloat16
F32 = jnp.float32
PLANE = ("z", "x")
DP = ("z", "x", "near")
MP = ("far", "core")
SMEM = pltpu.SMEM


def dot(left_side, right_side, left_dim=1, right_dim=0):
    return lax.dot_general(
        left_side, right_side, (((left_dim,), (right_dim,)), ((), ())), preferred_element_type=F32
    )


def call(body, outs, scratch=(), place=pltpu.VMEM, limit=12 << 20, cost=1000, aliases=(), far=()):
    def run(*arrays):
        space = pl.BlockSpec() if place is None else pl.BlockSpec(memory_space=place)
        apart = pl.BlockSpec(memory_space=pltpu.HBM)
        count = len(arrays)
        return pl.pallas_call(
            body,
            out_shape=[jax.ShapeDtypeStruct(s, d) for s, d in outs],
            in_specs=[apart if i in far else space for i in range(count)],
            out_specs=[apart if count + i in far else space for i in range(len(outs))],
            scratch_shapes=[pltpu.VMEM(*s) if isinstance(s, tuple) else s for s in scratch],
            cost_estimate=pl.CostEstimate(flops=cost, bytes_accessed=1000, transcendentals=0),
            compiler_params=pltpu.CompilerParams(vmem_limit_bytes=limit),
            input_output_aliases=dict(aliases),
            name=body.__name__,
        )(*arrays)

    return run


def line(ref):
    return ref[...].reshape(1, -1)


def norm_parts(values_in):
    center = values_in - jnp.mean(values_in, axis=-1, keepdims=True)
    spread = jnp.mean(center * center, axis=-1, keepdims=True)
    inverse = lax.rsqrt(spread + EPSILON)
    return center * inverse, inverse


def norm_back(grad, xhat, inverse, gain):
    scaled = grad * gain
    centre = jnp.mean(scaled, axis=-1, keepdims=True)
    along = jnp.mean(scaled * xhat, axis=-1, keepdims=True)
    return inverse * (scaled - centre - xhat * along)


def half_at(which, half):
    core = lax.axis_index("core")
    return pl.multiple_of((core if which == 0 else 1 - core) * half, half)


def fold(rows):
    return jnp.sum(rows, axis=0, keepdims=True)


def attend_kernel(
    lens_ref,
    tok_ref,
    gain_ref,
    shift_ref,
    w_ref,
    bias_ref,
    out_ref,
    normed_out,
    qkv_out,
    probs_out,
    ctx_out,
    own_out,
    other_out,
    normed_ref,
    qkv_ref,
    probs_ref,
    ctx_ref,
    own_ref,
    other_ref,
    lens_at,
    tok_at,
    gain_at,
    shift_at,
    w_at,
    bias_at,
    out_at,
    semaphores,
):
    length, features = tok_ref.shape
    half = length // 2
    heads = bias_ref.shape[0]
    size = bias_ref.shape[1] // 2
    copies = []

    def fetch(source, target):
        copies.append(pltpu.make_async_copy(source, target, semaphores.at[len(copies)]))
        copies[-1].start()
        return copies[-1]

    piece = half // 2
    pieces = []
    for which in range(2):
        for part in range(2):
            start = half_at(which, half) + part * piece
            at = which * half + part * piece
            pieces.append(fetch(tok_ref.at[pl.ds(start, piece)], tok_at.at[pl.ds(at, piece)]))
    norms = [fetch(gain_ref, gain_at), fetch(shift_ref, shift_at)]
    weights = []
    for head in range(heads):
        rows = pl.ds(head * 3 * size, 3 * size)
        weights.append(fetch(w_ref.at[rows], w_at.at[rows]))
    bias_copy, lens_copy = fetch(bias_ref, bias_at), fetch(lens_ref, lens_at)
    out_copy = fetch(out_ref, out_at)
    for copy in norms:
        copy.wait()
    step = 64
    for index, copy in enumerate(pieces):
        copy.wait()
        for first in range(index * piece, (index + 1) * piece, step):
            xhat, _ = norm_parts(tok_at[first : first + step, :].astype(F32))
            normed_ref[first : first + step, :] = (xhat * line(gain_at) + line(shift_at)).astype(BF)
    leaving = [fetch(normed_ref, normed_out)]
    bias_copy.wait()
    lens_copy.wait()
    lens_ref, bias_ref, w_ref = lens_at, bias_at, w_at

    diagonal = lax.broadcasted_iota(jnp.int32, (2 * size, 2 * size), 0) == (
        lax.broadcasted_iota(jnp.int32, (2 * size, 2 * size), 1)
    )
    for head in range(heads):
        base = head * 3 * size
        column = jnp.sum(
            jnp.where(diagonal, bias_ref[head : head + 1, :], 0.0), axis=1, keepdims=True
        )
        weights[head].wait()
        projected = dot(w_ref[base : base + 3 * size, :], normed_ref[...], 1, 1)
        qkv_ref[base : base + size, :] = (projected[:size] + column[:size]).astype(BF)
        qkv_ref[base + size : base + 2 * size, :] = projected[size : 2 * size].astype(BF)
        qkv_ref[base + 2 * size : base + 3 * size, :] = (
            projected[2 * size :] + column[size:]
        ).astype(BF)
    leaving.append(fetch(qkv_ref, qkv_out))

    docs = lens_ref.shape[1]
    ends = [lens_ref[0, 0]]
    for doc in range(1, docs):
        ends.append(ends[-1] + lens_ref[0, doc])

    def numbers(shape, dim, first):
        place = lax.broadcasted_iota(jnp.int32, shape, dim) + first + lax.axis_index("core") * half
        place = jnp.where(place >= length, place - length, place)
        number = jnp.zeros(shape, jnp.int32)
        for end in ends:
            number += (place >= end).astype(jnp.int32)
        return jnp.where(number >= docs, docs + place, number)

    key_docs = numbers((1, length), 1, 0)
    block = 128
    query_docs = [numbers((block, 1), 0, first) for first in range(0, length, block)]
    scale = size ** (-0.5)
    for head in range(heads):
        base = head * 3 * size
        keys = qkv_ref[base + size : base + 2 * size, :]
        for index in range(length // block):
            rows = slice(index * block, (index + 1) * block)
            scores = dot(qkv_ref[base : base + size, rows], keys, 0, 0) * scale
            scores = jnp.where(query_docs[index] == key_docs, scores, MASKED)
            expo = jnp.exp(scores - jnp.max(scores, axis=-1, keepdims=True))
            probs = expo * (1.0 / jnp.sum(expo, axis=-1, keepdims=True))
            probs_ref[head, rows, :] = probs.astype(BF)
        leaving.append(fetch(probs_ref.at[head], probs_out.at[head]))
        values = qkv_ref[base + 2 * size : base + 3 * size, :]
        ctx_ref[head * size : (head + 1) * size, :] = dot(values, probs_ref[head], 1, 1).astype(BF)
    leaving.append(fetch(ctx_ref, ctx_out))
    out_copy.wait()
    other_ref[...] = dot(ctx_ref[:, half:], out_at[...], 0, 0).astype(BF)
    leaving.append(fetch(other_ref, other_out))
    own_ref[...] = dot(ctx_ref[:, :half], out_at[...], 0, 0).astype(BF)
    leaving.append(fetch(own_ref, own_out))
    for copy in leaving:
        copy.wait()


def resid_kernel(tok_ref, pair_ref, come_ref, bias_ref, gain_ref, shift_ref, normed_ref, resid_ref):
    half = pair_ref.shape[0]
    start = half_at(0, half)
    step = 64
    for first in range(0, half, step):
        rows = slice(first, first + step)
        resid = (
            tok_ref[pl.ds(start + first, step), :].astype(F32)
            + (pair_ref[rows, :].astype(F32) + come_ref[rows, :].astype(F32))
            + line(bias_ref)
        )
        resid_ref[rows, :] = resid
        xhat, _ = norm_parts(resid)
        normed_ref[rows, :] = (xhat * line(gain_ref) + line(shift_ref)).astype(BF)


def expert_kernel(
    mine_ref,
    theirs_ref,
    up_ref,
    bias_ref,
    down_ref,
    cot_ref,
    hidden_ref,
    grad_ref,
    own_ref,
    other_ref,
    sum_ref,
):
    half = mine_ref.shape[0]
    step = 128
    total = jnp.zeros((1, up_ref.shape[1]), F32)
    for which in (1, 0):
        start = half_at(which, half)
        for first in range(0, half, step):
            rows = slice(first, first + step)
            normed = (theirs_ref if which else mine_ref)[rows, :]
            pre = dot(normed, up_ref[...]) + line(bias_ref)
            back = dot(cot_ref[pl.ds(start + first, step), :], down_ref[...], 1, 1)
            cumulative = 0.5 * (1.0 + lax.erf(pre * 0.7071067811865476))
            at = slice(which * half + first, which * half + first + step)
            hidden_ref[at, :] = (pre * cumulative).astype(BF)
            slope = cumulative + pre * (jnp.exp(-0.5 * pre * pre) * 0.3989422804014327)
            grad = (back * slope).astype(BF)
            grad_ref[at, :] = grad
            total += fold(grad.astype(F32))
            part = dot(grad, up_ref[...], 1, 1)
            (other_ref if which else own_ref)[rows, :] = part.astype(BF)
    sum_ref[...] = total


def expert_weights_kernel(hidden_ref, cot_ref, mine_ref, theirs_ref, grad_ref, chunk_ref):
    half = mine_ref.shape[0]
    count, pair, _ = chunk_ref.shape
    each = pair // 2
    cot_mine = cot_ref[pl.ds(half_at(0, half), half), :]
    cot_theirs = cot_ref[pl.ds(half_at(1, half), half), :]
    some = 4
    for first in range(0, count, some):
        columns = slice(first * each, (first + some) * each)
        down = dot(hidden_ref[:half, columns], cot_mine, 0, 0)
        down += dot(hidden_ref[half:, columns], cot_theirs, 0, 0)
        chunk_ref[first : first + some, :each, :] = down.astype(BF).reshape(some, each, -1)
        up = dot(mine_ref[:, columns], grad_ref[:half, :], 0, 0)
        up += dot(theirs_ref[:, columns], grad_ref[half:, :], 0, 0)
        chunk_ref[first : first + some, each:, :] = up.astype(BF).reshape(some, each, -1)


def second_norm_kernel(
    pair_ref, come_ref, resid_ref, gain_ref, cot_ref, low_ref, grad_ref, rows_ref
):
    half = resid_ref.shape[0]
    start = half_at(0, half)
    step = 64
    gains, shifts, outs, downs = 0.0, 0.0, 0.0, 0.0
    for first in range(0, half, step):
        rows = slice(first, first + step)
        xhat, inverse = norm_parts(resid_ref[rows, :])
        grad = pair_ref[rows, :].astype(F32) + come_ref[rows, :].astype(F32)
        cot = cot_ref[pl.ds(start + first, step), :].astype(F32)
        back = cot + norm_back(grad, xhat, inverse, line(gain_ref))
        grad_ref[rows, :] = back
        low = back.astype(BF)
        low_ref[rows, :] = low
        gains += fold(grad * xhat)
        shifts += fold(grad)
        outs += fold(low.astype(F32))
        downs += fold(cot)
    rows_ref[...] = jnp.zeros_like(rows_ref)
    for index, value in ((2, gains), (3, shifts), (4, outs), (5, downs)):
        rows_ref[index : index + 1, :] = value


def attend_back_kernel(
    mine_ref,
    theirs_ref,
    out_ref,
    probs_ref,
    qkv_ref,
    ctx_ref,
    normed_ref,
    grads_ref,
    chunk_ref,
    sums_ref,
    back_ref,
    score_ref,
):
    heads, length, _ = probs_ref.shape
    half = length // 2
    size = ctx_ref.shape[0] // heads
    scale = size ** (-0.5)
    back_ref[:, :half] = dot(out_ref[...], mine_ref[...], 1, 1).astype(BF)
    back_ref[:, half:] = dot(out_ref[...], theirs_ref[...], 1, 1).astype(BF)
    block = 128
    for head in range(heads):
        base = head * 3 * size
        own = slice(head * size, (head + 1) * size)
        queries = qkv_ref[base : base + size, :]
        keys = qkv_ref[base + size : base + 2 * size, :]
        values = qkv_ref[base + 2 * size : base + 3 * size, :]
        for first in range(0, length, block):
            rows = slice(first, first + block)
            probs = probs_ref[head, rows, :].astype(F32)
            probs_grad = dot(back_ref[own, rows], values, 0, 0)
            centre = jnp.sum(probs_grad * probs, axis=-1, keepdims=True)
            score_ref[rows, :] = (probs * (probs_grad - centre)).astype(BF)
        score_grad = score_ref[...]
        grads_ref[base : base + size, :] = (dot(keys, score_grad, 1, 1) * scale).astype(BF)
        grads_ref[base + size : base + 2 * size, :] = (dot(queries, score_grad) * scale).astype(BF)
        grads_ref[base + 2 * size : base + 3 * size, :] = dot(
            back_ref[own, :], probs_ref[head]
        ).astype(BF)
    width = grads_ref.shape[0]
    each = chunk_ref.shape[1]
    some = 4
    for first in range(0, width, some * each):
        grad = dot(grads_ref[first : first + some * each, :], normed_ref[...]).astype(BF)
        at = first // each
        chunk_ref[at : at + some] = grad.reshape(some, each, -1)
    outs = dot(ctx_ref[:, :half], mine_ref[...]) + dot(ctx_ref[:, half:], theirs_ref[...])
    chunk_ref[width // each :] = outs.astype(BF).reshape(-1, each, outs.shape[1])
    sums_ref[...] = dot(jnp.ones((8, length), BF), grads_ref[...], 1, 1)


def attend_in_kernel(grads_ref, w_ref, own_ref, other_ref):
    half = own_ref.shape[0]
    other_ref[...] = dot(grads_ref[:, half:], w_ref[...], 0, 0).astype(BF)
    own_ref[...] = dot(grads_ref[:, :half], w_ref[...], 0, 0).astype(BF)


def expert_out_kernel(hidden_ref, down_ref, own_ref, other_ref):
    half = own_ref.shape[0]
    other_ref[...] = dot(hidden_ref[half:, :], down_ref[...]).astype(BF)
    own_ref[...] = dot(hidden_ref[:half, :], down_ref[...]).astype(BF)


def mixed_kernel(resid_ref, pair_ref, come_ref, bias_ref, mixed_ref):
    total = pair_ref[...].astype(F32) + come_ref[...].astype(F32)
    mixed_ref[...] = (resid_ref[...] + total + line(bias_ref)).astype(BF)


def first_norm_kernel(tok_ref, pair_ref, come_ref, gain_ref, back_ref, rows_ref, grad_ref):
    half = pair_ref.shape[0]
    start = half_at(0, half)
    step = 64
    gains, shifts = 0.0, 0.0
    for first in range(0, half, step):
        rows = slice(first, first + step)
        xhat, inverse = norm_parts(tok_ref[pl.ds(start + first, step), :].astype(F32))
        grad = pair_ref[rows, :].astype(F32) + come_ref[rows, :].astype(F32)
        grad_ref[rows, :] = back_ref[rows, :] + norm_back(grad, xhat, inverse, line(gain_ref))
        gains += fold(grad * xhat)
        shifts += fold(grad)
    grad_ref[half:, :] = rows_ref[...]
    grad_ref[half : half + 1, :] = gains
    grad_ref[half + 1 : half + 2, :] = shifts


def mixed_order_kernel(mine_ref, theirs_ref, row_ref):
    half = mine_ref.shape[0]
    row_ref[pl.ds(half_at(0, half), half), :] = mine_ref[...]
    row_ref[pl.ds(half_at(1, half), half), :] = theirs_ref[...]


def token_order_kernel(mine_ref, theirs_ref, up_ref, qkv_ref, row_ref, whole_ref):
    half = row_ref.shape[0] // 2
    row_ref[pl.ds(half_at(0, half), half), :] = mine_ref[:half, :]
    row_ref[pl.ds(half_at(1, half), half), :] = theirs_ref[:half, :]
    whole_ref[...] = mine_ref[half:, :] + theirs_ref[half:, :]
    whole_ref[6:7, :] = up_ref[...]
    whole_ref[7:8, : qkv_ref.shape[1]] = qkv_ref[0:1, :]


def pair_kernel(own_ref, come_ref, pair_ref):
    pair_ref[...] = own_ref[...] + come_ref[...]


def expert_finish_kernel(pair_ref, come_ref, a_ref, b_ref):
    split = a_ref.shape[0]
    a_ref[...] = pair_ref[:split, :] + come_ref[:split, :]
    b_ref[...] = pair_ref[split:, :] + come_ref[split:, :]


def total_kernel(parts_ref, total_ref):
    step = 16
    for first in range(0, total_ref.shape[0], step):
        rows = slice(first, first + step)
        total = parts_ref[0, rows, :].astype(F32)
        for part in range(1, parts_ref.shape[0]):
            total += parts_ref[part, rows, :].astype(F32)
        total_ref[rows, :] = total.astype(BF)


def attend_total_kernel(parts_ref, whole_ref, pair_ref):
    count = parts_ref.shape[1]
    total_kernel(parts_ref, pair_ref.at[:count])
    pair_ref[count:, :] = whole_ref[...].astype(BF)


def place(axis, blocks, store):
    count = len(blocks)
    for shift, block in enumerate(blocks):
        store(lax.rem(lax.axis_index(axis) + count - shift, count), block)


def join(axis, bit, own_ref, come_ref, store):
    place = (lax.axis_index(axis) >> bit) & 1
    store(place, own_ref)
    store(1 - place, come_ref)


def join_kernel(axes, bit, *refs):
    count = len(axes)
    for index, axis in enumerate(axes):
        own_ref, come_ref, row_ref = refs[index], refs[count + index], refs[2 * count + index]
        each = own_ref.shape[0]

        def store(place, block, row_ref=row_ref, each=each):
            row_ref[pl.ds(pl.multiple_of(place * each, each), each), :] = block[...]

        join(axis, bit, own_ref, come_ref, store)


def expert_most_kernel(*refs):
    a_blocks, b_blocks, (down_ref, up_ref) = refs[:3], refs[3:6], refs[6:]
    rows = a_blocks[0].shape[0]
    planes = down_ref.shape[0] // rows
    each = rows // planes
    for shift, a_block, b_block in zip((0, 1, 3), a_blocks, b_blocks):
        source = lax.rem(lax.axis_index("x") + planes - shift, planes)
        for z in range(planes):
            at = pl.multiple_of(z * rows + source * each, each)
            down_ref[pl.ds(at, each), :] = a_block[z * each : (z + 1) * each, :].astype(F32)
        source = lax.rem(lax.axis_index("z") + planes - shift, planes)
        up_ref[pl.ds(pl.multiple_of(source * rows, rows), rows), :] = b_block[...].astype(F32)


def attend_finish_kernel(pair_ref, come_ref, copies_ref):
    total = pair_ref[...] + come_ref[...]
    for copy in range(copies_ref.shape[0]):
        copies_ref[copy] = total


def last_kernel(parts_ref, a_ref, b_ref, down_in, up_in, down_ref, up_ref, qkv_ref, out_ref, qv_ref, *refs):
    *vector_refs, a_full, b_full, semaphores = refs
    rows = a_ref.shape[0]
    side = down_ref.shape[0] // rows
    a_full[...] = a_ref[...].astype(F32)
    leaving = []
    source = lax.rem(lax.axis_index("x") + 2, side)
    for z in range(side):
        at = pl.multiple_of((z * side + source) * (rows // side), rows // side)
        leaving.append(
            pltpu.make_async_copy(
                a_full.at[pl.ds(z * (rows // side), rows // side)],
                down_ref.at[pl.ds(at, rows // side)],
                semaphores.at[z],
            )
        )
        leaving[-1].start()
    b_full[...] = b_ref[...].astype(F32)
    at = pl.multiple_of(lax.rem(lax.axis_index("z") + 2, side) * rows, rows)
    leaving.append(
        pltpu.make_async_copy(b_full, up_ref.at[pl.ds(at, rows)], semaphores.at[side])
    )
    leaving[-1].start()
    planes = parts_ref.shape[0]
    each = parts_ref.shape[1] - len(vector_refs) - 1
    width = qkv_ref.shape[0]
    total = jnp.zeros(parts_ref.shape[2:], F32)
    for part in range(planes):
        rows = parts_ref[part, :each, :].astype(F32)
        at = part * each
        if at < width:
            qkv_ref[at : at + each, :] = rows
        else:
            out_ref[at - width : at - width + each, :] = rows
        total = total + parts_ref[part, each:, :].astype(F32)
    for index, vector_ref in enumerate(vector_refs):
        vector_ref[...] = total[index]
    heads, double = qv_ref.shape
    size = double // 2
    for head in range(heads):
        base = 3 * head * size
        qv_ref[head : head + 1, :size] = total[7:8, base : base + size]
        qv_ref[head : head + 1, size:] = total[7:8, base + 2 * size : base + 3 * size]
    for copy in leaving:
        copy.wait()


def shards(
    tokens,
    segment_lens,
    norm1_gain,
    norm1_shift,
    qkv_weight,
    qv_bias,
    out_weight,
    out_bias,
    norm2_gain,
    norm2_shift,
    up_weight,
    up_bias,
    down_weight,
    down_bias,
    cotangent,
):
    length, features = tokens.shape[1:]
    heads = qkv_weight.shape[1]
    size = qkv_weight.shape[2] // 3
    width = heads * 3 * size
    units = up_weight.shape[1]
    half = length // 2
    plane = lax.axis_size(PLANE)
    side = lax.axis_size("x")
    tok, cot = tokens[0], cotangent[0]
    qkv_rows = qkv_weight.transpose(1, 2, 0).reshape(width, features)

    def core_swap(array_in):
        return lax.ppermute(array_in, "core", [(0, 1), (1, 0)])

    def chip_swap(array_in):
        return lax.ppermute(array_in, "far", [(0, 1), (1, 0)])

    def near_swap(array_in):
        return lax.ppermute(array_in, "near", [(0, 1), (1, 0)])

    def add_pair(own, other):
        return call(pair_kernel, ((other.shape, BF),))(own, core_swap(other))[0]

    def scatter(chunks):
        return lax.all_to_all(chunks, PLANE, 0, 0, tiled=True)

    def plane_sum(received):
        return call(total_kernel, ((received.shape[1:], BF),))(received)[0]

    def exchange(block, axis, bit):
        partner = (lambda i: i ^ 1) if bit == 0 else (lambda i: side - 1 - i)
        return lax.ppermute(block, axis, [(i, partner(i)) for i in range(side)])

    def joiner(axes, bit):
        def kernel(*refs):
            join_kernel(axes, bit, *refs)

        kernel.__name__ = "join_kernel"
        return kernel

    def along(block, axis):
        moves = [[(i, (i + shift) % side) for i in range(side)] for shift in range(1, side)]
        far, near, back = (lax.ppermute(block, axis, moves[i]) for i in (1, 0, 2))
        return (block, near, far, back)

    half_low, half_full = ((half, features), BF), ((half, features), F32)
    row_low, row_full = ((length, features), BF), ((length, features), F32)
    rows_full = ((8, features), F32)
    count = heads * size

    outs = (
        row_low,
        ((width, length), BF),
        ((heads, length, length), BF),
        ((count, length), BF),
        half_low,
        half_low,
    )
    staged = (
        pltpu.SMEM(segment_lens.shape, segment_lens.dtype),
        row_low,
        ((features,), F32),
        ((features,), F32),
        ((width, features), BF),
        (qv_bias.shape, F32),
        (out_weight.shape, BF),
        pltpu.SemaphoreType.DMA((14 + 2 * heads,)),
    )
    normed_one, qkv, probs, context, own, other = call(
        attend_kernel, outs, outs + staged, pltpu.HBM, 60 << 20
    )(segment_lens, tok, norm1_gain, norm1_shift, qkv_rows, qv_bias, out_weight)
    pair = add_pair(own, other)
    normed_mine, resid = call(resid_kernel, (half_low, half_full))(
        tok, pair, chip_swap(pair), out_bias, norm2_gain, norm2_shift
    )
    normed_theirs = core_swap(normed_mine)

    hidden, up_grad, own, other, up_sums = call(
        expert_kernel,
        (((length, units), BF), ((length, units), BF), half_low, half_low, ((1, units), F32)),
    )(normed_mine, normed_theirs, up_weight, up_bias, down_weight, cot)
    pair = add_pair(own, other)
    pair, hidden = lax.optimization_barrier((pair, hidden))
    (chunks,) = call(
        expert_weights_kernel,
        (((plane, (units + features) // plane, features), BF),),
        cost=20_000_000_000,
    )(hidden, cot, normed_mine, normed_theirs, up_grad)
    come = chip_swap(pair)
    expert_parts = scatter(chunks)
    own, other = call(expert_out_kernel, (half_low, half_low))(hidden, down_weight)
    other, _ = lax.optimization_barrier((other, come))
    mixed_pair = add_pair(own, other)
    mixed_come = chip_swap(mixed_pair)
    low_mine, resid_grad, sums = call(second_norm_kernel, (half_low, half_full, rows_full))(
        pair, come, resid, norm2_gain, cot
    )
    low_theirs = core_swap(low_mine)

    qkv_grad, chunks, qkv_sums = call(
        attend_back_kernel,
        (((width, length), BF), ((plane, (width + count) // plane, features), BF), ((8, width), F32)),
        (((count, length), BF), ((length, length), BF)),
    )(low_mine, low_theirs, out_weight, probs, qkv, context, normed_one)
    attend_parts = scatter(chunks)
    qkv_grad, mixed_come = lax.optimization_barrier((qkv_grad, mixed_come))
    own, other = call(attend_in_kernel, (half_low, half_low))(qkv_grad, qkv_rows)
    parts_pair = add_pair(own, other)

    come = chip_swap(parts_pair)
    pair = plane_sum(expert_parts)
    each = pair.shape[0] // 2
    near_pair, come = lax.optimization_barrier((near_swap(pair), come))
    blocks = call(expert_finish_kernel, (((each, features), BF),) * 2)(pair, near_pair)
    (token_grad,) = call(first_norm_kernel, (((half + 8, features), F32),))(
        tok, parts_pair, come, norm1_gain, resid_grad, sums
    )
    tokens_grad, whole = call(token_order_kernel, (row_full, rows_full))(
        token_grad, core_swap(token_grad), up_sums, qkv_sums
    )
    step = (exchange(blocks[0], "z", 0), exchange(blocks[1], "x", 0))
    blocks = call(joiner(("z", "x"), 0), (((2 * each, features), BF),) * 2)(*blocks, *step)
    rows = attend_parts.shape[1] + whole.shape[0]
    blocks, whole = lax.optimization_barrier((blocks, whole))
    (pair,) = call(attend_total_kernel, (((rows, features), BF),))(attend_parts, whole)
    blocks, pair = lax.optimization_barrier((blocks, pair))
    step = (exchange(blocks[0], "z", 1), exchange(blocks[1], "x", 1))
    blocks = call(joiner(("z", "x"), 1), (((4 * each, features), BF),) * 2)(*blocks, *step)
    down_blocks, up_blocks = along(blocks[0], "x"), along(blocks[1], "z")
    (mixed,) = call(mixed_kernel, (half_low,))(resid, mixed_pair, mixed_come, down_bias)
    (mixed,) = call(mixed_order_kernel, (row_low,))(mixed, core_swap(mixed))

    rows = pair.shape[0]
    come = near_swap(pair)
    down_own, down_near, down_far, down_back = down_blocks
    up_own, up_near, up_far, up_back = up_blocks
    come, down_near, down_back, up_near, up_back = lax.optimization_barrier(
        (come, down_near, down_back, up_near, up_back)
    )
    (copies,) = call(attend_finish_kernel, (((plane, rows, features), BF),))(pair, come)
    gathered = scatter(copies)
    down_grad, up_weight_grad = call(
        expert_most_kernel,
        (((units, features), F32), ((features, units), F32)),
        place=None,
        limit=60 << 20,
    )(down_own, down_near, down_back, up_own, up_near, up_back)
    block = down_far.shape
    down_grad, up_weight_grad, qkv_grads, out_weight_grad, qv_bias_grad, *vectors = call(
        last_kernel,
        (((units, features), F32), ((features, units), F32))
        + (((width, features), F32), ((count, features), F32), (qv_bias.shape, F32))
        + (((features,), F32),) * 7,
        ((block, F32), (block, F32), pltpu.SemaphoreType.DMA((1 + side,))),
        aliases=((3, 0), (4, 1)),
        far=(3, 4, 5, 6),
    )(gathered, down_far, up_far, down_grad, up_weight_grad)
    return (
        mixed[None],
        tokens_grad[None],
        vectors[0],
        vectors[1],
        qkv_grads.reshape(heads, 3 * size, features).transpose(2, 0, 1),
        qv_bias_grad,
        out_weight_grad,
        vectors[4],
        vectors[2],
        vectors[3],
        up_weight_grad,
        vectors[6],
        down_grad,
        vectors[5],
    )


def solution(mesh):
    fine = Mesh(mesh.devices.reshape(4, 4, 2, 2, 2), ("z", "x", "near", "far", "core"))
    rows, first, features = P(DP, None, None), P(MP, None), P(MP)
    weights = (
        P(),
        P(),
        P(None, MP, None),
        first,
        first,
        P(),
        P(),
        P(),
        P(None, MP),
        features,
        first,
        P(),
    )
    return jax.shard_map(
        shards,
        mesh=fine,
        in_specs=(rows, P(DP, None)) + weights + (rows,),
        out_specs=(rows, rows) + weights,
        check_vma=False,
    )
```

```python
import jax
import jax.numpy as jnp
from jax import lax
from jax.experimental import pallas as pl
from jax.experimental.pallas import tpu as pltpu
from jax.sharding import Mesh
from jax.sharding import PartitionSpec as P

EPSILON = 1e-05
MASKED = -1e30
BF = jnp.bfloat16
F32 = jnp.float32
PLANE = ("z", "x")
DP = ("z", "x", "near")
MP = ("far", "core")
SMEM = pltpu.SMEM


def dot(left_side, right_side, left_dim=1, right_dim=0):
    return lax.dot_general(
        left_side, right_side, (((left_dim,), (right_dim,)), ((), ())), preferred_element_type=F32
    )


def call(body, outs, scratch=(), place=pltpu.VMEM, limit=12 << 20, cost=1000, aliases=(), far=()):
    def run(*arrays):
        space = pl.BlockSpec() if place is None else pl.BlockSpec(memory_space=place)
        apart = pl.BlockSpec(memory_space=pltpu.HBM)
        count = len(arrays)
        return pl.pallas_call(
            body,
            out_shape=[jax.ShapeDtypeStruct(s, d) for s, d in outs],
            in_specs=[apart if i in far else space for i in range(count)],
            out_specs=[apart if count + i in far else space for i in range(len(outs))],
            scratch_shapes=[pltpu.VMEM(*s) if isinstance(s, tuple) else s for s in scratch],
            cost_estimate=pl.CostEstimate(flops=cost, bytes_accessed=1000, transcendentals=0),
            compiler_params=pltpu.CompilerParams(vmem_limit_bytes=limit),
            input_output_aliases=dict(aliases),
            name=body.__name__,
        )(*arrays)

    return run


def line(ref):
    return ref[...].reshape(1, -1)


def norm_parts(values_in):
    center = values_in - jnp.mean(values_in, axis=-1, keepdims=True)
    spread = jnp.mean(center * center, axis=-1, keepdims=True)
    inverse = lax.rsqrt(spread + EPSILON)
    return center * inverse, inverse


def norm_back(grad, xhat, inverse, gain):
    scaled = grad * gain
    centre = jnp.mean(scaled, axis=-1, keepdims=True)
    along = jnp.mean(scaled * xhat, axis=-1, keepdims=True)
    return inverse * (scaled - centre - xhat * along)


def half_at(which, half):
    core = lax.axis_index("core")
    return pl.multiple_of((core if which == 0 else 1 - core) * half, half)


def fold(rows):
    return jnp.sum(rows, axis=0, keepdims=True)


def attend_kernel(
    lens_ref,
    tok_ref,
    gain_ref,
    shift_ref,
    w_ref,
    bias_ref,
    out_ref,
    normed_out,
    qkv_out,
    probs_out,
    ctx_out,
    own_out,
    other_out,
    normed_ref,
    qkv_ref,
    probs_ref,
    ctx_ref,
    own_ref,
    other_ref,
    lens_at,
    tok_at,
    gain_at,
    shift_at,
    w_at,
    bias_at,
    out_at,
    semaphores,
):
    length, features = tok_ref.shape
    half = length // 2
    heads = bias_ref.shape[0]
    size = bias_ref.shape[1] // 2
    copies = []

    def fetch(source, target):
        copies.append(pltpu.make_async_copy(source, target, semaphores.at[len(copies)]))
        copies[-1].start()
        return copies[-1]

    piece = half // 2
    pieces = []
    for which in range(2):
        for part in range(2):
            start = half_at(which, half) + part * piece
            at = which * half + part * piece
            pieces.append(fetch(tok_ref.at[pl.ds(start, piece)], tok_at.at[pl.ds(at, piece)]))
    norms = [fetch(gain_ref, gain_at), fetch(shift_ref, shift_at)]
    weights = []
    for head in range(heads):
        rows = pl.ds(head * 3 * size, 3 * size)
        weights.append(fetch(w_ref.at[rows], w_at.at[rows]))
    bias_copy, lens_copy = fetch(bias_ref, bias_at), fetch(lens_ref, lens_at)
    out_copy = fetch(out_ref, out_at)
    for copy in norms:
        copy.wait()
    step = 64
    for index, copy in enumerate(pieces):
        copy.wait()
        for first in range(index * piece, (index + 1) * piece, step):
            xhat, _ = norm_parts(tok_at[first : first + step, :].astype(F32))
            normed_ref[first : first + step, :] = (xhat * line(gain_at) + line(shift_at)).astype(BF)
    leaving = [fetch(normed_ref, normed_out)]
    bias_copy.wait()
    lens_copy.wait()
    lens_ref, bias_ref, w_ref = lens_at, bias_at, w_at

    diagonal = lax.broadcasted_iota(jnp.int32, (2 * size, 2 * size), 0) == (
        lax.broadcasted_iota(jnp.int32, (2 * size, 2 * size), 1)
    )
    for head in range(heads):
        base = head * 3 * size
        column = jnp.sum(
            jnp.where(diagonal, bias_ref[head : head + 1, :], 0.0), axis=1, keepdims=True
        )
        weights[head].wait()
        projected = dot(w_ref[base : base + 3 * size, :], normed_ref[...], 1, 1)
        qkv_ref[base : base + size, :] = (projected[:size] + column[:size]).astype(BF)
        qkv_ref[base + size : base + 2 * size, :] = projected[size : 2 * size].astype(BF)
        qkv_ref[base + 2 * size : base + 3 * size, :] = (
            projected[2 * size :] + column[size:]
        ).astype(BF)
    leaving.append(fetch(qkv_ref, qkv_out))

    docs = lens_ref.shape[1]
    ends = [lens_ref[0, 0]]
    for doc in range(1, docs):
        ends.append(ends[-1] + lens_ref[0, doc])

    def numbers(shape, dim, first):
        place = lax.broadcasted_iota(jnp.int32, shape, dim) + first + lax.axis_index("core") * half
        place = jnp.where(place >= length, place - length, place)
        number = jnp.zeros(shape, jnp.int32)
        for end in ends:
            number += (place >= end).astype(jnp.int32)
        return jnp.where(number >= docs, docs + place, number)

    key_docs = numbers((1, length), 1, 0)
    block = 128
    query_docs = [numbers((block, 1), 0, first) for first in range(0, length, block)]
    scale = size ** (-0.5)
    for head in range(heads):
        base = head * 3 * size
        keys = qkv_ref[base + size : base + 2 * size, :]
        for index in range(length // block):
            rows = slice(index * block, (index + 1) * block)
            scores = dot(qkv_ref[base : base + size, rows], keys, 0, 0) * scale
            scores = jnp.where(query_docs[index] == key_docs, scores, MASKED)
            expo = jnp.exp(scores - jnp.max(scores, axis=-1, keepdims=True))
            probs = expo * (1.0 / jnp.sum(expo, axis=-1, keepdims=True))
            probs_ref[head, rows, :] = probs.astype(BF)
        leaving.append(fetch(probs_ref.at[head], probs_out.at[head]))
        values = qkv_ref[base + 2 * size : base + 3 * size, :]
        ctx_ref[head * size : (head + 1) * size, :] = dot(values, probs_ref[head], 1, 1).astype(BF)
    leaving.append(fetch(ctx_ref, ctx_out))
    out_copy.wait()
    other_ref[...] = dot(ctx_ref[:, half:], out_at[...], 0, 0).astype(BF)
    leaving.append(fetch(other_ref, other_out))
    own_ref[...] = dot(ctx_ref[:, :half], out_at[...], 0, 0).astype(BF)
    leaving.append(fetch(own_ref, own_out))
    for copy in leaving:
        copy.wait()


def resid_kernel(tok_ref, pair_ref, come_ref, bias_ref, gain_ref, shift_ref, normed_ref, resid_ref):
    half = pair_ref.shape[0]
    start = half_at(0, half)
    step = 64
    for first in range(0, half, step):
        rows = slice(first, first + step)
        resid = (
            tok_ref[pl.ds(start + first, step), :].astype(F32)
            + (pair_ref[rows, :].astype(F32) + come_ref[rows, :].astype(F32))
            + line(bias_ref)
        )
        resid_ref[rows, :] = resid
        xhat, _ = norm_parts(resid)
        normed_ref[rows, :] = (xhat * line(gain_ref) + line(shift_ref)).astype(BF)


def expert_kernel(
    mine_ref,
    theirs_ref,
    up_ref,
    bias_ref,
    down_ref,
    cot_ref,
    hidden_ref,
    grad_ref,
    own_ref,
    other_ref,
    sum_ref,
):
    half = mine_ref.shape[0]
    step = 128
    total = jnp.zeros((1, up_ref.shape[1]), F32)
    for which in (1, 0):
        start = half_at(which, half)
        for first in range(0, half, step):
            rows = slice(first, first + step)
            normed = (theirs_ref if which else mine_ref)[rows, :]
            pre = dot(normed, up_ref[...]) + line(bias_ref)
            back = dot(cot_ref[pl.ds(start + first, step), :], down_ref[...], 1, 1)
            cumulative = 0.5 * (1.0 + lax.erf(pre * 0.7071067811865476))
            at = slice(which * half + first, which * half + first + step)
            hidden_ref[at, :] = (pre * cumulative).astype(BF)
            slope = cumulative + pre * (jnp.exp(-0.5 * pre * pre) * 0.3989422804014327)
            grad = (back * slope).astype(BF)
            grad_ref[at, :] = grad
            total += fold(grad.astype(F32))
            part = dot(grad, up_ref[...], 1, 1)
            (other_ref if which else own_ref)[rows, :] = part.astype(BF)
    sum_ref[...] = total


def expert_weights_kernel(hidden_ref, cot_ref, mine_ref, theirs_ref, grad_ref, chunk_ref):
    half = mine_ref.shape[0]
    count, pair, _ = chunk_ref.shape
    each = pair // 2
    cot_mine = cot_ref[pl.ds(half_at(0, half), half), :]
    cot_theirs = cot_ref[pl.ds(half_at(1, half), half), :]
    some = 4
    for first in range(0, count, some):
        columns = slice(first * each, (first + some) * each)
        down = dot(hidden_ref[:half, columns], cot_mine, 0, 0)
        down += dot(hidden_ref[half:, columns], cot_theirs, 0, 0)
        chunk_ref[first : first + some, :each, :] = down.astype(BF).reshape(some, each, -1)
        up = dot(mine_ref[:, columns], grad_ref[:half, :], 0, 0)
        up += dot(theirs_ref[:, columns], grad_ref[half:, :], 0, 0)
        chunk_ref[first : first + some, each:, :] = up.astype(BF).reshape(some, each, -1)


def second_norm_kernel(
    pair_ref, come_ref, resid_ref, gain_ref, cot_ref, low_ref, grad_ref, rows_ref
):
    half = resid_ref.shape[0]
    start = half_at(0, half)
    step = 64
    gains, shifts, outs, downs = 0.0, 0.0, 0.0, 0.0
    for first in range(0, half, step):
        rows = slice(first, first + step)
        xhat, inverse = norm_parts(resid_ref[rows, :])
        grad = pair_ref[rows, :].astype(F32) + come_ref[rows, :].astype(F32)
        cot = cot_ref[pl.ds(start + first, step), :].astype(F32)
        back = cot + norm_back(grad, xhat, inverse, line(gain_ref))
        grad_ref[rows, :] = back
        low = back.astype(BF)
        low_ref[rows, :] = low
        gains += fold(grad * xhat)
        shifts += fold(grad)
        outs += fold(low.astype(F32))
        downs += fold(cot)
    rows_ref[...] = jnp.zeros_like(rows_ref)
    for index, value in ((2, gains), (3, shifts), (4, outs), (5, downs)):
        rows_ref[index : index + 1, :] = value


def attend_back_kernel(
    mine_ref,
    theirs_ref,
    out_ref,
    probs_ref,
    qkv_ref,
    ctx_ref,
    normed_ref,
    grads_ref,
    chunk_ref,
    sums_ref,
    back_ref,
    score_ref,
):
    heads, length, _ = probs_ref.shape
    half = length // 2
    size = ctx_ref.shape[0] // heads
    scale = size ** (-0.5)
    back_ref[:, :half] = dot(out_ref[...], mine_ref[...], 1, 1).astype(BF)
    back_ref[:, half:] = dot(out_ref[...], theirs_ref[...], 1, 1).astype(BF)
    block = 128
    for head in range(heads):
        base = head * 3 * size
        own = slice(head * size, (head + 1) * size)
        queries = qkv_ref[base : base + size, :]
        keys = qkv_ref[base + size : base + 2 * size, :]
        values = qkv_ref[base + 2 * size : base + 3 * size, :]
        for first in range(0, length, block):
            rows = slice(first, first + block)
            probs = probs_ref[head, rows, :].astype(F32)
            probs_grad = dot(back_ref[own, rows], values, 0, 0)
            centre = jnp.sum(probs_grad * probs, axis=-1, keepdims=True)
            score_ref[rows, :] = (probs * (probs_grad - centre)).astype(BF)
        score_grad = score_ref[...]
        grads_ref[base : base + size, :] = (dot(keys, score_grad, 1, 1) * scale).astype(BF)
        grads_ref[base + size : base + 2 * size, :] = (dot(queries, score_grad) * scale).astype(BF)
        grads_ref[base + 2 * size : base + 3 * size, :] = dot(
            back_ref[own, :], probs_ref[head]
        ).astype(BF)
    width = grads_ref.shape[0]
    each = chunk_ref.shape[1]
    some = 4
    for first in range(0, width, some * each):
        grad = dot(grads_ref[first : first + some * each, :], normed_ref[...]).astype(BF)
        at = first // each
        chunk_ref[at : at + some] = grad.reshape(some, each, -1)
    outs = dot(ctx_ref[:, :half], mine_ref[...]) + dot(ctx_ref[:, half:], theirs_ref[...])
    chunk_ref[width // each :] = outs.astype(BF).reshape(-1, each, outs.shape[1])
    sums_ref[...] = dot(jnp.ones((8, length), BF), grads_ref[...], 1, 1)


def attend_in_kernel(grads_ref, w_ref, own_ref, other_ref):
    half = own_ref.shape[0]
    other_ref[...] = dot(grads_ref[:, half:], w_ref[...], 0, 0).astype(BF)
    own_ref[...] = dot(grads_ref[:, :half], w_ref[...], 0, 0).astype(BF)


def expert_out_kernel(hidden_ref, down_ref, own_ref, other_ref):
    half = own_ref.shape[0]
    other_ref[...] = dot(hidden_ref[half:, :], down_ref[...]).astype(BF)
    own_ref[...] = dot(hidden_ref[:half, :], down_ref[...]).astype(BF)


def mixed_kernel(resid_ref, pair_ref, come_ref, bias_ref, mixed_ref):
    total = pair_ref[...].astype(F32) + come_ref[...].astype(F32)
    mixed_ref[...] = (resid_ref[...] + total + line(bias_ref)).astype(BF)


def first_norm_kernel(tok_ref, pair_ref, come_ref, gain_ref, back_ref, rows_ref, grad_ref):
    half = pair_ref.shape[0]
    start = half_at(0, half)
    step = 64
    gains, shifts = 0.0, 0.0
    for first in range(0, half, step):
        rows = slice(first, first + step)
        xhat, inverse = norm_parts(tok_ref[pl.ds(start + first, step), :].astype(F32))
        grad = pair_ref[rows, :].astype(F32) + come_ref[rows, :].astype(F32)
        grad_ref[rows, :] = back_ref[rows, :] + norm_back(grad, xhat, inverse, line(gain_ref))
        gains += fold(grad * xhat)
        shifts += fold(grad)
    grad_ref[half:, :] = rows_ref[...]
    grad_ref[half : half + 1, :] = gains
    grad_ref[half + 1 : half + 2, :] = shifts


def mixed_order_kernel(mine_ref, theirs_ref, row_ref):
    half = mine_ref.shape[0]
    row_ref[pl.ds(half_at(0, half), half), :] = mine_ref[...]
    row_ref[pl.ds(half_at(1, half), half), :] = theirs_ref[...]


def token_order_kernel(mine_ref, theirs_ref, up_ref, qkv_ref, row_ref, whole_ref):
    half = row_ref.shape[0] // 2
    row_ref[pl.ds(half_at(0, half), half), :] = mine_ref[:half, :]
    row_ref[pl.ds(half_at(1, half), half), :] = theirs_ref[:half, :]
    whole_ref[...] = mine_ref[half:, :] + theirs_ref[half:, :]
    whole_ref[6:7, :] = up_ref[...]
    whole_ref[7:8, : qkv_ref.shape[1]] = qkv_ref[0:1, :]


def pair_kernel(own_ref, come_ref, pair_ref):
    pair_ref[...] = own_ref[...] + come_ref[...]


def expert_finish_kernel(pair_ref, come_ref, a_ref, b_ref):
    split = a_ref.shape[0]
    a_ref[...] = pair_ref[:split, :] + come_ref[:split, :]
    b_ref[...] = pair_ref[split:, :] + come_ref[split:, :]


def total_kernel(parts_ref, total_ref):
    step = 16
    for first in range(0, total_ref.shape[0], step):
        rows = slice(first, first + step)
        total = parts_ref[0, rows, :].astype(F32)
        for part in range(1, parts_ref.shape[0]):
            total += parts_ref[part, rows, :].astype(F32)
        total_ref[rows, :] = total.astype(BF)


def attend_total_kernel(parts_ref, whole_ref, pair_ref):
    count = parts_ref.shape[1]
    total_kernel(parts_ref, pair_ref.at[:count])
    pair_ref[count:, :] = whole_ref[...].astype(BF)


def place(axis, blocks, store):
    count = len(blocks)
    for shift, block in enumerate(blocks):
        store(lax.rem(lax.axis_index(axis) + count - shift, count), block)


def join(axis, bit, own_ref, come_ref, store):
    place = (lax.axis_index(axis) >> bit) & 1
    store(place, own_ref)
    store(1 - place, come_ref)


def join_kernel(axes, bit, *refs):
    count = len(axes)
    for index, axis in enumerate(axes):
        own_ref, come_ref, row_ref = refs[index], refs[count + index], refs[2 * count + index]
        each = own_ref.shape[0]

        def store(place, block, row_ref=row_ref, each=each):
            row_ref[pl.ds(pl.multiple_of(place * each, each), each), :] = block[...]

        join(axis, bit, own_ref, come_ref, store)


def expert_most_kernel(*refs):
    a_blocks, b_blocks, (down_ref, up_ref) = refs[:3], refs[3:6], refs[6:]
    rows = a_blocks[0].shape[0]
    planes = down_ref.shape[0] // rows
    each = rows // planes
    for shift, a_block, b_block in zip((0, 1, 3), a_blocks, b_blocks):
        source = lax.rem(lax.axis_index("x") + planes - shift, planes)
        for z in range(planes):
            at = pl.multiple_of(z * rows + source * each, each)
            down_ref[pl.ds(at, each), :] = a_block[z * each : (z + 1) * each, :].astype(F32)
        source = lax.rem(lax.axis_index("z") + planes - shift, planes)
        up_ref[pl.ds(pl.multiple_of(source * rows, rows), rows), :] = b_block[...].astype(F32)


def attend_finish_kernel(pair_ref, come_ref, copies_ref):
    total = pair_ref[...] + come_ref[...]
    for copy in range(copies_ref.shape[0]):
        copies_ref[copy] = total


def last_kernel(parts_ref, a_low, a_high, b_low, b_high, down_in, up_in, down_ref, up_ref, qkv_ref, out_ref, qv_ref, *refs):
    *vector_refs, a_full, b_full, semaphores = refs
    half = a_low.shape[0]
    rows = 2 * half
    side = down_ref.shape[0] // rows
    a_full[:half, :] = a_low[...].astype(F32)
    a_full[half:, :] = a_high[...].astype(F32)
    leaving = []
    source = lax.rem(lax.axis_index("x") + 2, side)
    for z in range(side):
        at = pl.multiple_of((z * side + source) * (rows // side), rows // side)
        leaving.append(
            pltpu.make_async_copy(
                a_full.at[pl.ds(z * (rows // side), rows // side)],
                down_ref.at[pl.ds(at, rows // side)],
                semaphores.at[z],
            )
        )
        leaving[-1].start()
    b_full[:half, :] = b_low[...].astype(F32)
    b_full[half:, :] = b_high[...].astype(F32)
    at = pl.multiple_of(lax.rem(lax.axis_index("z") + 2, side) * rows, rows)
    leaving.append(
        pltpu.make_async_copy(b_full, up_ref.at[pl.ds(at, rows)], semaphores.at[side])
    )
    leaving[-1].start()
    planes = parts_ref.shape[0]
    each = parts_ref.shape[1] - len(vector_refs) - 1
    width = qkv_ref.shape[0]
    total = jnp.zeros(parts_ref.shape[2:], F32)
    for part in range(planes):
        rows = parts_ref[part, :each, :].astype(F32)
        at = part * each
        if at < width:
            qkv_ref[at : at + each, :] = rows
        else:
            out_ref[at - width : at - width + each, :] = rows
        total = total + parts_ref[part, each:, :].astype(F32)
    for index, vector_ref in enumerate(vector_refs):
        vector_ref[...] = total[index]
    heads, double = qv_ref.shape
    size = double // 2
    for head in range(heads):
        base = 3 * head * size
        qv_ref[head : head + 1, :size] = total[7:8, base : base + size]
        qv_ref[head : head + 1, size:] = total[7:8, base + 2 * size : base + 3 * size]
    for copy in leaving:
        copy.wait()


def shards(
    tokens,
    segment_lens,
    norm1_gain,
    norm1_shift,
    qkv_weight,
    qv_bias,
    out_weight,
    out_bias,
    norm2_gain,
    norm2_shift,
    up_weight,
    up_bias,
    down_weight,
    down_bias,
    cotangent,
):
    length, features = tokens.shape[1:]
    heads = qkv_weight.shape[1]
    size = qkv_weight.shape[2] // 3
    width = heads * 3 * size
    units = up_weight.shape[1]
    half = length // 2
    plane = lax.axis_size(PLANE)
    side = lax.axis_size("x")
    tok, cot = tokens[0], cotangent[0]
    qkv_rows = qkv_weight.transpose(1, 2, 0).reshape(width, features)

    def core_swap(array_in):
        return lax.ppermute(array_in, "core", [(0, 1), (1, 0)])

    def chip_swap(array_in):
        return lax.ppermute(array_in, "far", [(0, 1), (1, 0)])

    def near_swap(array_in):
        return lax.ppermute(array_in, "near", [(0, 1), (1, 0)])

    def add_pair(own, other):
        return call(pair_kernel, ((other.shape, BF),))(own, core_swap(other))[0]

    def scatter(chunks):
        return lax.all_to_all(chunks, PLANE, 0, 0, tiled=True)

    def plane_sum(received):
        return call(total_kernel, ((received.shape[1:], BF),))(received)[0]

    def exchange(block, axis, bit):
        partner = (lambda i: i ^ 1) if bit == 0 else (lambda i: side - 1 - i)
        return lax.ppermute(block, axis, [(i, partner(i)) for i in range(side)])

    def joiner(axes, bit):
        def kernel(*refs):
            join_kernel(axes, bit, *refs)

        kernel.__name__ = "join_kernel"
        return kernel

    def onward(block, axis, shift):
        return lax.ppermute(block, axis, [(i, (i + shift) % side) for i in range(side)])

    half_low, half_full = ((half, features), BF), ((half, features), F32)
    row_low, row_full = ((length, features), BF), ((length, features), F32)
    rows_full = ((8, features), F32)
    count = heads * size

    outs = (
        row_low,
        ((width, length), BF),
        ((heads, length, length), BF),
        ((count, length), BF),
        half_low,
        half_low,
    )
    staged = (
        pltpu.SMEM(segment_lens.shape, segment_lens.dtype),
        row_low,
        ((features,), F32),
        ((features,), F32),
        ((width, features), BF),
        (qv_bias.shape, F32),
        (out_weight.shape, BF),
        pltpu.SemaphoreType.DMA((14 + 2 * heads,)),
    )
    normed_one, qkv, probs, context, own, other = call(
        attend_kernel, outs, outs + staged, pltpu.HBM, 60 << 20
    )(segment_lens, tok, norm1_gain, norm1_shift, qkv_rows, qv_bias, out_weight)
    pair = add_pair(own, other)
    normed_mine, resid = call(resid_kernel, (half_low, half_full))(
        tok, pair, chip_swap(pair), out_bias, norm2_gain, norm2_shift
    )
    normed_theirs = core_swap(normed_mine)

    hidden, up_grad, own, other, up_sums = call(
        expert_kernel,
        (((length, units), BF), ((length, units), BF), half_low, half_low, ((1, units), F32)),
    )(normed_mine, normed_theirs, up_weight, up_bias, down_weight, cot)
    pair = add_pair(own, other)
    pair, hidden = lax.optimization_barrier((pair, hidden))
    (chunks,) = call(
        expert_weights_kernel,
        (((plane, (units + features) // plane, features), BF),),
        cost=20_000_000_000,
    )(hidden, cot, normed_mine, normed_theirs, up_grad)
    come = chip_swap(pair)
    expert_parts = scatter(chunks)
    own, other = call(expert_out_kernel, (half_low, half_low))(hidden, down_weight)
    other, _ = lax.optimization_barrier((other, come))
    mixed_pair = add_pair(own, other)
    mixed_come = chip_swap(mixed_pair)
    low_mine, resid_grad, sums = call(second_norm_kernel, (half_low, half_full, rows_full))(
        pair, come, resid, norm2_gain, cot
    )
    low_theirs = core_swap(low_mine)

    qkv_grad, chunks, qkv_sums = call(
        attend_back_kernel,
        (((width, length), BF), ((plane, (width + count) // plane, features), BF), ((8, width), F32)),
        (((count, length), BF), ((length, length), BF)),
    )(low_mine, low_theirs, out_weight, probs, qkv, context, normed_one)
    attend_parts = scatter(chunks)
    qkv_grad, mixed_come = lax.optimization_barrier((qkv_grad, mixed_come))
    own, other = call(attend_in_kernel, (half_low, half_low))(qkv_grad, qkv_rows)
    parts_pair = add_pair(own, other)

    come = chip_swap(parts_pair)
    pair = plane_sum(expert_parts)
    each = pair.shape[0] // 2
    near_pair, come = lax.optimization_barrier((near_swap(pair), come))
    blocks = call(expert_finish_kernel, (((each, features), BF),) * 2)(pair, near_pair)
    (token_grad,) = call(first_norm_kernel, (((half + 8, features), F32),))(
        tok, parts_pair, come, norm1_gain, resid_grad, sums
    )
    tokens_grad, whole = call(token_order_kernel, (row_full, rows_full))(
        token_grad, core_swap(token_grad), up_sums, qkv_sums
    )
    step = (exchange(blocks[0], "z", 0), exchange(blocks[1], "x", 0))
    blocks = call(joiner(("z", "x"), 0), (((2 * each, features), BF),) * 2)(*blocks, *step)
    rows = attend_parts.shape[1] + whole.shape[0]
    blocks, whole = lax.optimization_barrier((blocks, whole))
    (pair,) = call(attend_total_kernel, (((rows, features), BF),))(attend_parts, whole)
    blocks, pair = lax.optimization_barrier((blocks, pair))
    step = (exchange(blocks[0], "z", 1), exchange(blocks[1], "x", 1))
    blocks = call(joiner(("z", "x"), 1), (((4 * each, features), BF),) * 2)(*blocks, *step)
    down_own, up_own = blocks
    down_near, down_back = onward(down_own, "x", 1), onward(down_own, "x", side - 1)
    up_near, up_back = onward(up_own, "z", 1), onward(up_own, "z", side - 1)
    (mixed,) = call(mixed_kernel, (half_low,))(resid, mixed_pair, mixed_come, down_bias)
    (mixed,) = call(mixed_order_kernel, (row_low,))(mixed, core_swap(mixed))

    rows = pair.shape[0]
    come = near_swap(pair)
    come, down_near, down_back, up_near, up_back = lax.optimization_barrier(
        (come, down_near, down_back, up_near, up_back)
    )
    (copies,) = call(attend_finish_kernel, (((plane, rows, features), BF),))(pair, come)
    halves = (down_near[: 2 * each], down_back[2 * each :], up_near[: 2 * each], up_back[2 * each :])
    gathered = scatter(copies)
    down_grad, up_weight_grad = call(
        expert_most_kernel,
        (((units, features), F32), ((features, units), F32)),
        place=None,
        limit=60 << 20,
    )(down_own, down_near, down_back, up_own, up_near, up_back)
    far = (
        onward(halves[0], "x", 1),
        onward(halves[1], "x", side - 1),
        onward(halves[2], "z", 1),
        onward(halves[3], "z", side - 1),
    )
    block = down_own.shape
    down_grad, up_weight_grad, qkv_grads, out_weight_grad, qv_bias_grad, *vectors = call(
        last_kernel,
        (((units, features), F32), ((features, units), F32))
        + (((width, features), F32), ((count, features), F32), (qv_bias.shape, F32))
        + (((features,), F32),) * 7,
        ((block, F32), (block, F32), pltpu.SemaphoreType.DMA((1 + side,))),
        aliases=((5, 0), (6, 1)),
        far=(5, 6, 7, 8),
    )(gathered, *far, down_grad, up_weight_grad)
    return (
        mixed[None],
        tokens_grad[None],
        vectors[0],
        vectors[1],
        qkv_grads.reshape(heads, 3 * size, features).transpose(2, 0, 1),
        qv_bias_grad,
        out_weight_grad,
        vectors[4],
        vectors[2],
        vectors[3],
        up_weight_grad,
        vectors[6],
        down_grad,
        vectors[5],
    )


def solution(mesh):
    fine = Mesh(mesh.devices.reshape(4, 4, 2, 2, 2), ("z", "x", "near", "far", "core"))
    rows, first, features = P(DP, None, None), P(MP, None), P(MP)
    weights = (
        P(),
        P(),
        P(None, MP, None),
        first,
        first,
        P(),
        P(),
        P(),
        P(None, MP),
        features,
        first,
        P(),
    )
    return jax.shard_map(
        shards,
        mesh=fine,
        in_specs=(rows, P(DP, None)) + weights + (rows,),
        out_specs=(rows, rows) + weights,
        check_vma=False,
    )
```

```python
import jax
import jax.numpy as jnp
from jax import lax
from jax.experimental import pallas as pl
from jax.experimental.pallas import tpu as pltpu
from jax.sharding import Mesh
from jax.sharding import PartitionSpec as P

EPSILON = 1e-05
MASKED = -1e30
BF = jnp.bfloat16
F32 = jnp.float32
PLANE = ("z", "x")
DP = ("z", "x", "near")
MP = ("far", "core")
SMEM = pltpu.SMEM


def dot(left_side, right_side, left_dim=1, right_dim=0):
    return lax.dot_general(
        left_side, right_side, (((left_dim,), (right_dim,)), ((), ())), preferred_element_type=F32
    )


def call(body, outs, scratch=(), place=pltpu.VMEM, limit=12 << 20, cost=1000, aliases=(), far=()):
    def run(*arrays):
        space = pl.BlockSpec() if place is None else pl.BlockSpec(memory_space=place)
        apart = pl.BlockSpec(memory_space=pltpu.HBM)
        count = len(arrays)
        return pl.pallas_call(
            body,
            out_shape=[jax.ShapeDtypeStruct(s, d) for s, d in outs],
            in_specs=[apart if i in far else space for i in range(count)],
            out_specs=[apart if count + i in far else space for i in range(len(outs))],
            scratch_shapes=[pltpu.VMEM(*s) if isinstance(s, tuple) else s for s in scratch],
            cost_estimate=pl.CostEstimate(flops=cost, bytes_accessed=1000, transcendentals=0),
            compiler_params=pltpu.CompilerParams(vmem_limit_bytes=limit),
            input_output_aliases=dict(aliases),
            name=body.__name__,
        )(*arrays)

    return run


def line(ref):
    return ref[...].reshape(1, -1)


def norm_parts(values_in):
    center = values_in - jnp.mean(values_in, axis=-1, keepdims=True)
    spread = jnp.mean(center * center, axis=-1, keepdims=True)
    inverse = lax.rsqrt(spread + EPSILON)
    return center * inverse, inverse


def norm_back(grad, xhat, inverse, gain):
    scaled = grad * gain
    centre = jnp.mean(scaled, axis=-1, keepdims=True)
    along = jnp.mean(scaled * xhat, axis=-1, keepdims=True)
    return inverse * (scaled - centre - xhat * along)


def half_at(which, half):
    core = lax.axis_index("core")
    return pl.multiple_of((core if which == 0 else 1 - core) * half, half)


def fold(rows):
    return jnp.sum(rows, axis=0, keepdims=True)


def attend_kernel(
    lens_ref,
    tok_ref,
    gain_ref,
    shift_ref,
    w_ref,
    bias_ref,
    out_ref,
    normed_out,
    qkv_out,
    probs_out,
    ctx_out,
    own_out,
    other_out,
    normed_ref,
    qkv_ref,
    probs_ref,
    ctx_ref,
    own_ref,
    other_ref,
    lens_at,
    tok_at,
    gain_at,
    shift_at,
    w_at,
    bias_at,
    out_at,
    semaphores,
):
    length, features = tok_ref.shape
    half = length // 2
    heads = bias_ref.shape[0]
    size = bias_ref.shape[1] // 2
    copies = []

    def fetch(source, target):
        copies.append(pltpu.make_async_copy(source, target, semaphores.at[len(copies)]))
        copies[-1].start()
        return copies[-1]

    piece = half
    pieces = []
    for which in range(2):
        for part in range(1):
            start = half_at(which, half) + part * piece
            at = which * half + part * piece
            pieces.append(fetch(tok_ref.at[pl.ds(start, piece)], tok_at.at[pl.ds(at, piece)]))
    norms = [fetch(gain_ref, gain_at), fetch(shift_ref, shift_at)]
    weights = []
    for head in range(heads):
        rows = pl.ds(head * 3 * size, 3 * size)
        weights.append(fetch(w_ref.at[rows], w_at.at[rows]))
    bias_copy, lens_copy = fetch(bias_ref, bias_at), fetch(lens_ref, lens_at)
    out_copy = fetch(out_ref, out_at)
    for copy in norms:
        copy.wait()
    step = 64
    for index, copy in enumerate(pieces):
        copy.wait()
        for first in range(index * piece, (index + 1) * piece, step):
            xhat, _ = norm_parts(tok_at[first : first + step, :].astype(F32))
            normed_ref[first : first + step, :] = (xhat * line(gain_at) + line(shift_at)).astype(BF)
    leaving = [fetch(normed_ref, normed_out)]
    bias_copy.wait()
    lens_copy.wait()
    lens_ref, bias_ref, w_ref = lens_at, bias_at, w_at

    diagonal = lax.broadcasted_iota(jnp.int32, (2 * size, 2 * size), 0) == (
        lax.broadcasted_iota(jnp.int32, (2 * size, 2 * size), 1)
    )
    for head in range(heads):
        base = head * 3 * size
        column = jnp.sum(
            jnp.where(diagonal, bias_ref[head : head + 1, :], 0.0), axis=1, keepdims=True
        )
        weights[head].wait()
        projected = dot(w_ref[base : base + 3 * size, :], normed_ref[...], 1, 1)
        qkv_ref[base : base + size, :] = (projected[:size] + column[:size]).astype(BF)
        qkv_ref[base + size : base + 2 * size, :] = projected[size : 2 * size].astype(BF)
        qkv_ref[base + 2 * size : base + 3 * size, :] = (
            projected[2 * size :] + column[size:]
        ).astype(BF)
    leaving.append(fetch(qkv_ref, qkv_out))

    docs = lens_ref.shape[1]
    ends = [lens_ref[0, 0]]
    for doc in range(1, docs):
        ends.append(ends[-1] + lens_ref[0, doc])

    def numbers(shape, dim, first):
        place = lax.broadcasted_iota(jnp.int32, shape, dim) + first + lax.axis_index("core") * half
        place = jnp.where(place >= length, place - length, place)
        number = jnp.zeros(shape, jnp.int32)
        for end in ends:
            number += (place >= end).astype(jnp.int32)
        return jnp.where(number >= docs, docs + place, number)

    key_docs = numbers((1, length), 1, 0)
    block = 128
    query_docs = [numbers((block, 1), 0, first) for first in range(0, length, block)]
    scale = size ** (-0.5)
    for head in range(heads):
        base = head * 3 * size
        keys = qkv_ref[base + size : base + 2 * size, :]
        for index in range(length // block):
            rows = slice(index * block, (index + 1) * block)
            scores = dot(qkv_ref[base : base + size, rows], keys, 0, 0) * scale
            scores = jnp.where(query_docs[index] == key_docs, scores, MASKED)
            expo = jnp.exp(scores - jnp.max(scores, axis=-1, keepdims=True))
            probs = expo * (1.0 / jnp.sum(expo, axis=-1, keepdims=True))
            probs_ref[head, rows, :] = probs.astype(BF)
        leaving.append(fetch(probs_ref.at[head], probs_out.at[head]))
        values = qkv_ref[base + 2 * size : base + 3 * size, :]
        ctx_ref[head * size : (head + 1) * size, :] = dot(values, probs_ref[head], 1, 1).astype(BF)
    leaving.append(fetch(ctx_ref, ctx_out))
    out_copy.wait()
    other_ref[...] = dot(ctx_ref[:, half:], out_at[...], 0, 0).astype(BF)
    leaving.append(fetch(other_ref, other_out))
    own_ref[...] = dot(ctx_ref[:, :half], out_at[...], 0, 0).astype(BF)
    leaving.append(fetch(own_ref, own_out))
    for copy in leaving:
        copy.wait()


def resid_kernel(tok_ref, pair_ref, come_ref, bias_ref, gain_ref, shift_ref, normed_ref, resid_ref):
    half = pair_ref.shape[0]
    start = half_at(0, half)
    step = 64
    for first in range(0, half, step):
        rows = slice(first, first + step)
        resid = (
            tok_ref[pl.ds(start + first, step), :].astype(F32)
            + (pair_ref[rows, :].astype(F32) + come_ref[rows, :].astype(F32))
            + line(bias_ref)
        )
        resid_ref[rows, :] = resid
        xhat, _ = norm_parts(resid)
        normed_ref[rows, :] = (xhat * line(gain_ref) + line(shift_ref)).astype(BF)


def expert_kernel(
    mine_ref,
    theirs_ref,
    up_ref,
    bias_ref,
    down_ref,
    cot_ref,
    hidden_ref,
    grad_ref,
    own_ref,
    other_ref,
    sum_ref,
):
    half = mine_ref.shape[0]
    step = 128
    total = jnp.zeros((1, up_ref.shape[1]), F32)
    for which in (1, 0):
        start = half_at(which, half)
        for first in range(0, half, step):
            rows = slice(first, first + step)
            normed = (theirs_ref if which else mine_ref)[rows, :]
            pre = dot(normed, up_ref[...]) + line(bias_ref)
            back = dot(cot_ref[pl.ds(start + first, step), :], down_ref[...], 1, 1)
            cumulative = 0.5 * (1.0 + lax.erf(pre * 0.7071067811865476))
            at = slice(which * half + first, which * half + first + step)
            hidden_ref[at, :] = (pre * cumulative).astype(BF)
            slope = cumulative + pre * (jnp.exp(-0.5 * pre * pre) * 0.3989422804014327)
            grad = (back * slope).astype(BF)
            grad_ref[at, :] = grad
            total += fold(grad.astype(F32))
            part = dot(grad, up_ref[...], 1, 1)
            (other_ref if which else own_ref)[rows, :] = part.astype(BF)
    sum_ref[...] = total


def expert_weights_kernel(hidden_ref, cot_ref, mine_ref, theirs_ref, grad_ref, chunk_ref):
    half = mine_ref.shape[0]
    count, pair, _ = chunk_ref.shape
    each = pair // 2
    cot_mine = cot_ref[pl.ds(half_at(0, half), half), :]
    cot_theirs = cot_ref[pl.ds(half_at(1, half), half), :]
    some = 4
    for first in range(0, count, some):
        columns = slice(first * each, (first + some) * each)
        down = dot(hidden_ref[:half, columns], cot_mine, 0, 0)
        down += dot(hidden_ref[half:, columns], cot_theirs, 0, 0)
        chunk_ref[first : first + some, :each, :] = down.astype(BF).reshape(some, each, -1)
        up = dot(mine_ref[:, columns], grad_ref[:half, :], 0, 0)
        up += dot(theirs_ref[:, columns], grad_ref[half:, :], 0, 0)
        chunk_ref[first : first + some, each:, :] = up.astype(BF).reshape(some, each, -1)


def second_norm_kernel(
    pair_ref, come_ref, resid_ref, gain_ref, cot_ref, low_ref, grad_ref, rows_ref
):
    half = resid_ref.shape[0]
    start = half_at(0, half)
    step = 64
    gains, shifts, outs, downs = 0.0, 0.0, 0.0, 0.0
    for first in range(0, half, step):
        rows = slice(first, first + step)
        xhat, inverse = norm_parts(resid_ref[rows, :])
        grad = pair_ref[rows, :].astype(F32) + come_ref[rows, :].astype(F32)
        cot = cot_ref[pl.ds(start + first, step), :].astype(F32)
        back = cot + norm_back(grad, xhat, inverse, line(gain_ref))
        grad_ref[rows, :] = back
        low = back.astype(BF)
        low_ref[rows, :] = low
        gains += fold(grad * xhat)
        shifts += fold(grad)
        outs += fold(low.astype(F32))
        downs += fold(cot)
    rows_ref[...] = jnp.zeros_like(rows_ref)
    for index, value in ((2, gains), (3, shifts), (4, outs), (5, downs)):
        rows_ref[index : index + 1, :] = value


def attend_back_kernel(
    mine_ref,
    theirs_ref,
    out_ref,
    probs_ref,
    qkv_ref,
    ctx_ref,
    normed_ref,
    grads_ref,
    chunk_ref,
    sums_ref,
    back_ref,
    score_ref,
):
    heads, length, _ = probs_ref.shape
    half = length // 2
    size = ctx_ref.shape[0] // heads
    scale = size ** (-0.5)
    back_ref[:, :half] = dot(out_ref[...], mine_ref[...], 1, 1).astype(BF)
    back_ref[:, half:] = dot(out_ref[...], theirs_ref[...], 1, 1).astype(BF)
    block = 128
    for head in range(heads):
        base = head * 3 * size
        own = slice(head * size, (head + 1) * size)
        queries = qkv_ref[base : base + size, :]
        keys = qkv_ref[base + size : base + 2 * size, :]
        values = qkv_ref[base + 2 * size : base + 3 * size, :]
        for first in range(0, length, block):
            rows = slice(first, first + block)
            probs = probs_ref[head, rows, :].astype(F32)
            probs_grad = dot(back_ref[own, rows], values, 0, 0)
            centre = jnp.sum(probs_grad * probs, axis=-1, keepdims=True)
            score_ref[rows, :] = (probs * (probs_grad - centre)).astype(BF)
        score_grad = score_ref[...]
        grads_ref[base : base + size, :] = (dot(keys, score_grad, 1, 1) * scale).astype(BF)
        grads_ref[base + size : base + 2 * size, :] = (dot(queries, score_grad) * scale).astype(BF)
        grads_ref[base + 2 * size : base + 3 * size, :] = dot(
            back_ref[own, :], probs_ref[head]
        ).astype(BF)
    width = grads_ref.shape[0]
    each = chunk_ref.shape[1]
    some = 4
    for first in range(0, width, some * each):
        grad = dot(grads_ref[first : first + some * each, :], normed_ref[...]).astype(BF)
        at = first // each
        chunk_ref[at : at + some] = grad.reshape(some, each, -1)
    outs = dot(ctx_ref[:, :half], mine_ref[...]) + dot(ctx_ref[:, half:], theirs_ref[...])
    chunk_ref[width // each :] = outs.astype(BF).reshape(-1, each, outs.shape[1])
    sums_ref[...] = dot(jnp.ones((8, length), BF), grads_ref[...], 1, 1)


def attend_in_kernel(grads_ref, w_ref, own_ref, other_ref):
    half = own_ref.shape[0]
    other_ref[...] = dot(grads_ref[:, half:], w_ref[...], 0, 0).astype(BF)
    own_ref[...] = dot(grads_ref[:, :half], w_ref[...], 0, 0).astype(BF)


def expert_out_kernel(hidden_ref, down_ref, own_ref, other_ref):
    half = own_ref.shape[0]
    other_ref[...] = dot(hidden_ref[half:, :], down_ref[...]).astype(BF)
    own_ref[...] = dot(hidden_ref[:half, :], down_ref[...]).astype(BF)


def mixed_kernel(resid_ref, pair_ref, come_ref, bias_ref, mixed_ref):
    total = pair_ref[...].astype(F32) + come_ref[...].astype(F32)
    mixed_ref[...] = (resid_ref[...] + total + line(bias_ref)).astype(BF)


def first_norm_kernel(tok_ref, pair_ref, come_ref, gain_ref, back_ref, rows_ref, grad_ref):
    half = pair_ref.shape[0]
    start = half_at(0, half)
    step = 64
    gains, shifts = 0.0, 0.0
    for first in range(0, half, step):
        rows = slice(first, first + step)
        xhat, inverse = norm_parts(tok_ref[pl.ds(start + first, step), :].astype(F32))
        grad = pair_ref[rows, :].astype(F32) + come_ref[rows, :].astype(F32)
        grad_ref[rows, :] = back_ref[rows, :] + norm_back(grad, xhat, inverse, line(gain_ref))
        gains += fold(grad * xhat)
        shifts += fold(grad)
    grad_ref[half:, :] = rows_ref[...]
    grad_ref[half : half + 1, :] = gains
    grad_ref[half + 1 : half + 2, :] = shifts


def mixed_order_kernel(mine_ref, theirs_ref, row_ref):
    half = mine_ref.shape[0]
    row_ref[pl.ds(half_at(0, half), half), :] = mine_ref[...]
    row_ref[pl.ds(half_at(1, half), half), :] = theirs_ref[...]


def token_order_kernel(mine_ref, theirs_ref, up_ref, qkv_ref, row_ref, whole_ref):
    half = row_ref.shape[0] // 2
    row_ref[pl.ds(half_at(0, half), half), :] = mine_ref[:half, :]
    row_ref[pl.ds(half_at(1, half), half), :] = theirs_ref[:half, :]
    whole_ref[...] = mine_ref[half:, :] + theirs_ref[half:, :]
    whole_ref[6:7, :] = up_ref[...]
    whole_ref[7:8, : qkv_ref.shape[1]] = qkv_ref[0:1, :]


def pair_kernel(own_ref, come_ref, pair_ref):
    pair_ref[...] = own_ref[...] + come_ref[...]


def expert_finish_kernel(pair_ref, come_ref, a_ref, b_ref):
    split = a_ref.shape[0]
    a_ref[...] = pair_ref[:split, :] + come_ref[:split, :]
    b_ref[...] = pair_ref[split:, :] + come_ref[split:, :]


def total_kernel(parts_ref, total_ref):
    step = 16
    for first in range(0, total_ref.shape[0], step):
        rows = slice(first, first + step)
        total = parts_ref[0, rows, :].astype(F32)
        for part in range(1, parts_ref.shape[0]):
            total += parts_ref[part, rows, :].astype(F32)
        total_ref[rows, :] = total.astype(BF)


def attend_total_kernel(parts_ref, whole_ref, pair_ref):
    count = parts_ref.shape[1]
    total_kernel(parts_ref, pair_ref.at[:count])
    pair_ref[count:, :] = whole_ref[...].astype(BF)


def place(axis, blocks, store):
    count = len(blocks)
    for shift, block in enumerate(blocks):
        store(lax.rem(lax.axis_index(axis) + count - shift, count), block)


def join(axis, bit, own_ref, come_ref, store):
    place = (lax.axis_index(axis) >> bit) & 1
    store(place, own_ref)
    store(1 - place, come_ref)


def join_kernel(axes, bit, *refs):
    count = len(axes)
    for index, axis in enumerate(axes):
        own_ref, come_ref, row_ref = refs[index], refs[count + index], refs[2 * count + index]
        each = own_ref.shape[0]

        def store(place, block, row_ref=row_ref, each=each):
            row_ref[pl.ds(pl.multiple_of(place * each, each), each), :] = block[...]

        join(axis, bit, own_ref, come_ref, store)


def expert_most_kernel(*refs):
    a_blocks, b_blocks, (down_ref, up_ref) = refs[:3], refs[3:6], refs[6:]
    rows = a_blocks[0].shape[0]
    planes = down_ref.shape[0] // rows
    each = rows // planes
    for shift, a_block, b_block in zip((0, 1, 3), a_blocks, b_blocks):
        source = lax.rem(lax.axis_index("x") + planes - shift, planes)
        for z in range(planes):
            at = pl.multiple_of(z * rows + source * each, each)
            down_ref[pl.ds(at, each), :] = a_block[z * each : (z + 1) * each, :].astype(F32)
        source = lax.rem(lax.axis_index("z") + planes - shift, planes)
        up_ref[pl.ds(pl.multiple_of(source * rows, rows), rows), :] = b_block[...].astype(F32)


def attend_finish_kernel(pair_ref, come_ref, copies_ref):
    total = pair_ref[...] + come_ref[...]
    for copy in range(copies_ref.shape[0]):
        copies_ref[copy] = total


def last_kernel(parts_ref, a_low, a_high, b_low, b_high, down_in, up_in, down_ref, up_ref, qkv_ref, out_ref, qv_ref, *refs):
    *vector_refs, a_full, b_full, semaphores = refs
    half = a_low.shape[0]
    rows = 2 * half
    side = down_ref.shape[0] // rows
    a_full[:half, :] = a_low[...].astype(F32)
    a_full[half:, :] = a_high[...].astype(F32)
    leaving = []
    source = lax.rem(lax.axis_index("x") + 2, side)
    for z in range(side):
        at = pl.multiple_of((z * side + source) * (rows // side), rows // side)
        leaving.append(
            pltpu.make_async_copy(
                a_full.at[pl.ds(z * (rows // side), rows // side)],
                down_ref.at[pl.ds(at, rows // side)],
                semaphores.at[z],
            )
        )
        leaving[-1].start()
    b_full[:half, :] = b_low[...].astype(F32)
    b_full[half:, :] = b_high[...].astype(F32)
    at = pl.multiple_of(lax.rem(lax.axis_index("z") + 2, side) * rows, rows)
    leaving.append(
        pltpu.make_async_copy(b_full, up_ref.at[pl.ds(at, rows)], semaphores.at[side])
    )
    leaving[-1].start()
    planes = parts_ref.shape[0]
    each = parts_ref.shape[1] - len(vector_refs) - 1
    width = qkv_ref.shape[0]
    total = jnp.zeros(parts_ref.shape[2:], F32)
    for part in range(planes):
        rows = parts_ref[part, :each, :].astype(F32)
        at = part * each
        if at < width:
            qkv_ref[at : at + each, :] = rows
        else:
            out_ref[at - width : at - width + each, :] = rows
        total = total + parts_ref[part, each:, :].astype(F32)
    for index, vector_ref in enumerate(vector_refs):
        vector_ref[...] = total[index]
    heads, double = qv_ref.shape
    size = double // 2
    for head in range(heads):
        base = 3 * head * size
        qv_ref[head : head + 1, :size] = total[7:8, base : base + size]
        qv_ref[head : head + 1, size:] = total[7:8, base + 2 * size : base + 3 * size]
    for copy in leaving:
        copy.wait()


def shards(
    tokens,
    segment_lens,
    norm1_gain,
    norm1_shift,
    qkv_weight,
    qv_bias,
    out_weight,
    out_bias,
    norm2_gain,
    norm2_shift,
    up_weight,
    up_bias,
    down_weight,
    down_bias,
    cotangent,
):
    length, features = tokens.shape[1:]
    heads = qkv_weight.shape[1]
    size = qkv_weight.shape[2] // 3
    width = heads * 3 * size
    units = up_weight.shape[1]
    half = length // 2
    plane = lax.axis_size(PLANE)
    side = lax.axis_size("x")
    tok, cot = tokens[0], cotangent[0]
    qkv_rows = qkv_weight.transpose(1, 2, 0).reshape(width, features)

    def core_swap(array_in):
        return lax.ppermute(array_in, "core", [(0, 1), (1, 0)])

    def chip_swap(array_in):
        return lax.ppermute(array_in, "far", [(0, 1), (1, 0)])

    def near_swap(array_in):
        return lax.ppermute(array_in, "near", [(0, 1), (1, 0)])

    def add_pair(own, other):
        return call(pair_kernel, ((other.shape, BF),))(own, core_swap(other))[0]

    def scatter(chunks):
        return lax.all_to_all(chunks, PLANE, 0, 0, tiled=True)

    def plane_sum(received):
        return call(total_kernel, ((received.shape[1:], BF),))(received)[0]

    def exchange(block, axis, bit):
        partner = (lambda i: i ^ 1) if bit == 0 else (lambda i: side - 1 - i)
        return lax.ppermute(block, axis, [(i, partner(i)) for i in range(side)])

    def joiner(axes, bit):
        def kernel(*refs):
            join_kernel(axes, bit, *refs)

        kernel.__name__ = "join_kernel"
        return kernel

    def onward(block, axis, shift):
        return lax.ppermute(block, axis, [(i, (i + shift) % side) for i in range(side)])

    half_low, half_full = ((half, features), BF), ((half, features), F32)
    row_low, row_full = ((length, features), BF), ((length, features), F32)
    rows_full = ((8, features), F32)
    count = heads * size

    outs = (
        row_low,
        ((width, length), BF),
        ((heads, length, length), BF),
        ((count, length), BF),
        half_low,
        half_low,
    )
    staged = (
        pltpu.SMEM(segment_lens.shape, segment_lens.dtype),
        row_low,
        ((features,), F32),
        ((features,), F32),
        ((width, features), BF),
        (qv_bias.shape, F32),
        (out_weight.shape, BF),
        pltpu.SemaphoreType.DMA((14 + 2 * heads,)),
    )
    normed_one, qkv, probs, context, own, other = call(
        attend_kernel, outs, outs + staged, pltpu.HBM, 60 << 20
    )(segment_lens, tok, norm1_gain, norm1_shift, qkv_rows, qv_bias, out_weight)
    pair = add_pair(own, other)
    normed_mine, resid = call(resid_kernel, (half_low, half_full))(
        tok, pair, chip_swap(pair), out_bias, norm2_gain, norm2_shift
    )
    normed_theirs = core_swap(normed_mine)

    hidden, up_grad, own, other, up_sums = call(
        expert_kernel,
        (((length, units), BF), ((length, units), BF), half_low, half_low, ((1, units), F32)),
    )(normed_mine, normed_theirs, up_weight, up_bias, down_weight, cot)
    pair = add_pair(own, other)
    pair, hidden = lax.optimization_barrier((pair, hidden))
    (chunks,) = call(
        expert_weights_kernel,
        (((plane, (units + features) // plane, features), BF),),
        cost=20_000_000_000,
    )(hidden, cot, normed_mine, normed_theirs, up_grad)
    come = chip_swap(pair)
    expert_parts = scatter(chunks)
    own, other = call(expert_out_kernel, (half_low, half_low))(hidden, down_weight)
    other, _ = lax.optimization_barrier((other, come))
    mixed_pair = add_pair(own, other)
    mixed_come = chip_swap(mixed_pair)
    low_mine, resid_grad, sums = call(second_norm_kernel, (half_low, half_full, rows_full))(
        pair, come, resid, norm2_gain, cot
    )
    low_theirs = core_swap(low_mine)

    qkv_grad, chunks, qkv_sums = call(
        attend_back_kernel,
        (((width, length), BF), ((plane, (width + count) // plane, features), BF), ((8, width), F32)),
        (((count, length), BF), ((length, length), BF)),
    )(low_mine, low_theirs, out_weight, probs, qkv, context, normed_one)
    attend_parts = scatter(chunks)
    qkv_grad, mixed_come = lax.optimization_barrier((qkv_grad, mixed_come))
    own, other = call(attend_in_kernel, (half_low, half_low))(qkv_grad, qkv_rows)
    parts_pair = add_pair(own, other)

    come = chip_swap(parts_pair)
    pair = plane_sum(expert_parts)
    each = pair.shape[0] // 2
    near_pair, come = lax.optimization_barrier((near_swap(pair), come))
    blocks = call(expert_finish_kernel, (((each, features), BF),) * 2)(pair, near_pair)
    (token_grad,) = call(first_norm_kernel, (((half + 8, features), F32),))(
        tok, parts_pair, come, norm1_gain, resid_grad, sums
    )
    tokens_grad, whole = call(token_order_kernel, (row_full, rows_full))(
        token_grad, core_swap(token_grad), up_sums, qkv_sums
    )
    step = (exchange(blocks[0], "z", 0), exchange(blocks[1], "x", 0))
    blocks = call(joiner(("z", "x"), 0), (((2 * each, features), BF),) * 2)(*blocks, *step)
    rows = attend_parts.shape[1] + whole.shape[0]
    blocks, whole = lax.optimization_barrier((blocks, whole))
    (pair,) = call(attend_total_kernel, (((rows, features), BF),))(attend_parts, whole)
    blocks, pair = lax.optimization_barrier((blocks, pair))
    step = (exchange(blocks[0], "z", 1), exchange(blocks[1], "x", 1))
    blocks = call(joiner(("z", "x"), 1), (((4 * each, features), BF),) * 2)(*blocks, *step)
    down_own, up_own = blocks
    down_near, down_back = onward(down_own, "x", 1), onward(down_own, "x", side - 1)
    up_near, up_back = onward(up_own, "z", 1), onward(up_own, "z", side - 1)
    (mixed,) = call(mixed_kernel, (half_low,))(resid, mixed_pair, mixed_come, down_bias)
    (mixed,) = call(mixed_order_kernel, (row_low,))(mixed, core_swap(mixed))

    rows = pair.shape[0]
    come = near_swap(pair)
    come, down_near, down_back, up_near, up_back = lax.optimization_barrier(
        (come, down_near, down_back, up_near, up_back)
    )
    (copies,) = call(attend_finish_kernel, (((plane, rows, features), BF),))(pair, come)
    halves = (down_near[: 2 * each], down_back[2 * each :], up_near[: 2 * each], up_back[2 * each :])
    gathered = scatter(copies)
    down_grad, up_weight_grad = call(
        expert_most_kernel,
        (((units, features), F32), ((features, units), F32)),
        place=None,
        limit=60 << 20,
    )(down_own, down_near, down_back, up_own, up_near, up_back)
    far = (
        onward(halves[0], "x", 1),
        onward(halves[1], "x", side - 1),
        onward(halves[2], "z", 1),
        onward(halves[3], "z", side - 1),
    )
    block = down_own.shape
    down_grad, up_weight_grad, qkv_grads, out_weight_grad, qv_bias_grad, *vectors = call(
        last_kernel,
        (((units, features), F32), ((features, units), F32))
        + (((width, features), F32), ((count, features), F32), (qv_bias.shape, F32))
        + (((features,), F32),) * 7,
        ((block, F32), (block, F32), pltpu.SemaphoreType.DMA((1 + side,))),
        aliases=((5, 0), (6, 1)),
        far=(5, 6, 7, 8),
    )(gathered, *far, down_grad, up_weight_grad)
    return (
        mixed[None],
        tokens_grad[None],
        vectors[0],
        vectors[1],
        qkv_grads.reshape(heads, 3 * size, features).transpose(2, 0, 1),
        qv_bias_grad,
        out_weight_grad,
        vectors[4],
        vectors[2],
        vectors[3],
        up_weight_grad,
        vectors[6],
        down_grad,
        vectors[5],
    )


def solution(mesh):
    fine = Mesh(mesh.devices.reshape(4, 4, 2, 2, 2), ("z", "x", "near", "far", "core"))
    rows, first, features = P(DP, None, None), P(MP, None), P(MP)
    weights = (
        P(),
        P(),
        P(None, MP, None),
        first,
        first,
        P(),
        P(),
        P(),
        P(None, MP),
        features,
        first,
        P(),
    )
    return jax.shard_map(
        shards,
        mesh=fine,
        in_specs=(rows, P(DP, None)) + weights + (rows,),
        out_specs=(rows, rows) + weights,
        check_vma=False,
    )
```
